512 devices in a mesh: dp: 4 (over x), ctx: 32 (over y_lo, z, core), tp: 4 (over y_hi).
Axes of the slice: x: 4, y: 8 (y_hi: 4, y_lo: 2; y = y_hi * 2 + y_lo), z: 8, core: 2. Of those that a mesh axis runs over, the one named last changes fastest.
Arguments:
- upstream: bfloat16 [16384, 3072], P(('dp', 'ctx'), 'tp'), may hold values from -6 to 6
- router_logits: float32 [16384, 2], P(('dp', 'ctx')), may hold values from -6 to 6
- expert_ids: int32 [16384, 2], P(('dp', 'ctx')), may hold values from 0 to 7, all different within a row; in each aligned block of 128 rows (0 to 127, 128 to 255, ...) at most 36 rows name the same one
- hidden_saved: bfloat16 [4608, 65536], P('dp', ('ctx', 'tp')), may hold values from -0.75 to 0.75
- down_weight: bfloat16 [65536, 3072], P(('ctx', 'tp'), 'dp'), may hold values from -0.0625 to 0.0625
Outputs:
- hidden_grad: bfloat16 [4608, 65536], P('dp', ('ctx', 'tp'))
- down_grad: bfloat16 [65536, 3072], P(('ctx', 'tp'), 'dp')
- logit_grad: float32 [16384, 2], P(('dp', 'ctx'))
The draws below stay inside these ranges and needn't reach their ends.
Inputs may be any that keep to these rules, and one draw needn't show every extreme that they name: `expert_ids`: the ids of a row differ; in each aligned block of 128 rows (the rows of one device) no expert is named more than 36 times.
All inputs are finite; a program needn't handle non-finite values.
Results may differ from the reference program's by a relative error of at most 0.013.
Values may be sent and summed in bfloat16 or wider, within the bound.
No kernel may reach another device: no remote copies, remote signals or barrier semaphores. Data moves between devices by JAX's collectives and lax.ppermute only.
A program may use at most 128 MiB of HBM per device.

```python
import math
import jax
import jax.numpy as jnp
import numpy as np
from jax import lax

D = 3072
FF = 8192
EXPERTS = 8
TOP = 2
TOK_DEV = 128
CAP = 36
SLOTS = 1152
TOKENS = 16384
N_DP = 4
N_CTX = 32


def block_levels(stream_key, extent, shards, least, top_value):
    def one(dim, shards_of):
        draws = jax.random.uniform(jax.random.fold_in(jax.random.fold_in(stream_key, 6), dim), (shards_of,), jnp.float32, least / len(shards), top_value / len(shards))
        return jnp.repeat(jnp.exp(draws), extent[dim] // shards_of).reshape((-1,) + (1,) * (len(extent) - dim - 1))

    factor_of = one(*shards[0])
    for cut in shards[1:]:
        factor_of = factor_of * one(*cut)
    return factor_of


def routed_block(key, own, number, rows, number_of, top, reach, slope):
    order = jax.random.permutation(key, number_of)
    crowded, usual = load_shares(number_of, rows * top, reach, slope, True), load_shares(number_of, rows * top, reach, slope, False)
    places = jnp.arange(number_of)

    def named(tallies, turn):
        used = int((tallies > 0).sum())
        fixed = max(1, used // 4)
        shifted = fixed + (places - fixed + turn * (used - fixed)) % max(1, number_of - fixed)
        return jnp.zeros((number_of,), jnp.int32).at[order[jnp.where(places < fixed, places, shifted)]].set(jnp.asarray(tallies, jnp.int32))

    tallies = jnp.where(number % 4 == 0, named(crowded, number // 4), named(usual, number - number // 4 - 1))
    mixed = jax.random.permutation(jax.random.fold_in(own, 3), number_of)
    donor, taker = mixed[0:number_of // 2 * 2:2], mixed[1:number_of // 2 * 2:2]
    room = jnp.minimum(tallies[donor] - 1, reach - tallies[taker]) // 2
    room = jnp.where((donor == order[0]) | (taker == order[0]) | (tallies[taker] == 0), 0, jnp.maximum(room, 0))
    shifted = jax.random.randint(jax.random.fold_in(own, 4), (number_of // 2,), 0, 1 << 20) % (room + 1)
    tallies = tallies.at[donor].add(-shifted).at[taker].add(shifted)
    labels = jnp.searchsorted(jnp.cumsum(tallies), jnp.arange(rows * top), side="right").astype(jnp.int32)
    table = labels.reshape(top, rows).T
    table = table[jax.random.permutation(jax.random.fold_in(own, 1), rows)]
    turn = jax.random.randint(jax.random.fold_in(own, 2), (rows, 1), 0, top)
    return jnp.take_along_axis(table, (jnp.arange(top)[None, :] + turn) % top, axis=1)


def load_shares(amount, total, reach, lean, full):
    loads = [(1 << 20) // math.isqrt(rank ** lean) + 1 for rank in range(1, amount + 1)]
    largest = reach if full else min(reach, max(-(-total // amount), total * loads[0] // sum(loads)))
    least = 1 if total - largest >= amount - 1 else 0
    given, spare = [largest] + [least] * (amount - 1), total - largest - least * (amount - 1)
    while spare > 0:
        candidates = [i for i in range(1, amount) if given[i] < largest] or [i for i in range(1, amount) if given[i] < reach]
        pool, budget = sum([loads[i] for i in candidates]), spare
        for i in candidates:
            more = min(reach - given[i], max(1, budget * loads[i] // pool), spare)
            given[i] = given[i] + more
            spare = spare - more
    return np.array(given)


def noise(stream_key, extent, width, reach, pieces=(), held_as=jnp.bfloat16):
    gain = block_levels(stream_key, extent, pieces, -0.22, 0.18) if pieces else 1.0
    result = jax.random.normal(stream_key, extent, jnp.float32) * width * gain
    return jnp.minimum(jnp.maximum(result, -reach), reach).astype(held_as)


def setup_inputs(seed: int = 0) -> dict:
    arg_keys = jax.random.split(jax.random.key(seed), 6)
    upstream = noise(arg_keys[0], (TOKENS, D), 1.0, 6.0, ((0, 128), (1, 4)))
    router_logits = noise(arg_keys[1], (TOKENS, TOP), 1.0, 6.0, ((0, 128),), jnp.float32)
    expert_ids_keys = jax.random.split(jax.random.fold_in(arg_keys[2], 1), TOKENS // TOK_DEV)
    expert_ids_turns = jax.random.permutation(jax.random.fold_in(arg_keys[2], 3), TOKENS // TOK_DEV)
    expert_ids = jax.vmap(lambda own, number: routed_block(jax.random.fold_in(arg_keys[2], 2), own, number, TOK_DEV, EXPERTS, TOP, CAP, 1))(expert_ids_keys, expert_ids_turns).reshape((TOKENS, TOP))
    hidden_saved = noise(arg_keys[3], (N_DP * SLOTS, EXPERTS * FF), 0.125, 0.75, ((0, 4), (1, 128)))
    down_weight = noise(arg_keys[4], (EXPERTS * FF, D), FF ** -0.5, 0.0625, ((0, 128), (1, 4)))
    return dict(upstream=upstream, router_logits=router_logits, expert_ids=expert_ids, hidden_saved=hidden_saved, down_weight=down_weight)


def reference(upstream, router_logits, expert_ids, hidden_saved, down_weight):
    gates = 1.0 / (1.0 + jnp.exp(router_logits[:, ::-1] - router_logits))
    gates_sent = gates.astype(jnp.bfloat16)
    block_count = N_DP * N_CTX
    slots_all = N_CTX * CAP
    routes = expert_ids.reshape(block_count, TOK_DEV * TOP)
    onehot = (routes[:, :, None] == jnp.arange(EXPERTS, dtype=jnp.int32)[None, None, :]).astype(jnp.int32)
    earlier = jnp.cumsum(onehot, axis=1) - onehot
    slot = jnp.sum(earlier * onehot, axis=2).astype(jnp.int32)
    block_ids = jnp.arange(block_count, dtype=jnp.int32)[:, None]
    sequence = block_ids // N_CTX
    context = block_ids % N_CTX
    position = (((sequence * EXPERTS + routes) * N_CTX + context) * CAP + slot).astype(jnp.int32)
    route_index = (block_ids * (TOK_DEV * TOP) + jnp.arange(TOK_DEV * TOP, dtype=jnp.int32)[None, :]).astype(jnp.int32)
    sentinel = TOKENS * TOP
    table = jnp.full((N_DP * EXPERTS * slots_all,), sentinel, jnp.int32)
    table = table.at[position.reshape(-1)].set(route_index.reshape(-1))
    padded_rows = jnp.concatenate([upstream, jnp.zeros((1, D), jnp.bfloat16)], axis=0)
    padded_gates = jnp.concatenate([gates_sent.reshape(-1), jnp.zeros((1,), jnp.bfloat16)], axis=0)

    def per_expert(expert):
        weight = lax.dynamic_slice_in_dim(down_weight, expert * FF, FF, 0)
        weight_total = jnp.zeros((FF, D), jnp.float32)
        grads = []
        partials = []
        for sequence_id in range(N_DP):
            start = (sequence_id * EXPERTS + expert) * slots_all
            index = lax.dynamic_slice_in_dim(table, start, slots_all, 0)
            rows = padded_rows[index // TOP]
            gate_rows = padded_gates[index].astype(jnp.float32)[:, None]
            proj = lax.dot_general(rows, weight, (((1,), (1,)), ((), ())), preferred_element_type=jnp.float32)
            saved = lax.dynamic_slice_in_dim(
                lax.dynamic_slice_in_dim(hidden_saved, sequence_id * slots_all, slots_all, 0), expert * FF, FF, 1)
            grads.append((gate_rows * proj).astype(jnp.bfloat16))
            weighted = (gate_rows * rows.astype(jnp.float32)).astype(jnp.bfloat16)
            product = lax.dot_general(saved, weighted, (((0,), (0,)), ((), ())), preferred_element_type=jnp.float32)
            weight_total = weight_total + lax.optimization_barrier(product.astype(jnp.bfloat16)).astype(jnp.float32)
            partials.append(jnp.sum(saved.astype(jnp.float32) * proj, axis=1))
        return jnp.stack(grads), weight_total.astype(jnp.bfloat16), jnp.stack(partials)

    grads, weights, partials = lax.map(per_expert, jnp.arange(EXPERTS, dtype=jnp.int32))
    hidden_grad = grads.transpose(1, 2, 0, 3).reshape(N_DP * slots_all, EXPERTS * FF)
    down_grad = weights.reshape(EXPERTS * FF, D)
    flat_parts = partials.transpose(1, 0, 2).reshape(-1)
    route_grad = jnp.zeros((sentinel + 1,), jnp.float32).at[table].add(flat_parts)
    route_grad = route_grad[:sentinel].reshape(TOKENS, TOP)
    logit_grad = gates * (route_grad - jnp.sum(gates * route_grad, axis=1, keepdims=True))
    return hidden_grad, down_grad, logit_grad
```

```python
import jax
import jax.numpy as jnp
from jax import lax
from jax.experimental import pallas as pl
from jax.experimental.pallas import tpu as pltpu
from jax.sharding import PartitionSpec as P

EXPERTS = 8
TOP = 2
QUADS = 4
VMEM_LIMIT = 56 * 1024 * 1024


def compare_dot(a, b):
    return lax.dot_general(a, b, (((1,), (1,)), ((), ())), preferred_element_type=jnp.float32)


def pack_kernel(ids_ref, logits_ref, upstream_ref, packed_ref, position_ref, gates_ref):
    tokens = upstream_ref.shape[0]
    rows = packed_ref.shape[0]
    per_quad = rows // (EXPERTS * QUADS)
    slots = per_quad - 1
    capacity = slots * QUADS
    ids = [ids_ref[k : k + 1, :] for k in range(TOP)]
    expert = lax.broadcasted_iota(jnp.int32, (EXPERTS, tokens), 0)
    chosen = [(expert == ids[k]).astype(jnp.float32) for k in range(TOP)]
    before = (
        lax.broadcasted_iota(jnp.int32, (tokens, tokens), 0)
        < lax.broadcasted_iota(jnp.int32, (tokens, tokens), 1)
    ).astype(jnp.bfloat16)
    earlier = jnp.dot(
        (chosen[0] + chosen[1]).astype(jnp.bfloat16), before, preferred_element_type=jnp.float32
    )
    row = lax.broadcasted_iota(jnp.int32, (rows, tokens), 0)
    column = lax.broadcasted_iota(jnp.int32, (128, tokens), 0)
    place = jnp.zeros((rows, tokens), jnp.float32)
    gate_block = jnp.zeros((rows, 128), jnp.float32)
    for k in range(TOP):
        slot = jnp.sum(earlier * chosen[k], axis=0, keepdims=True).astype(jnp.int32)
        gate = 1.0 / (1.0 + jnp.exp(logits_ref[1 - k : 2 - k, :] - logits_ref[k : k + 1, :]))
        quad = sum((slot >= slots * i).astype(jnp.int32) for i in range(1, QUADS))
        within = slot - quad * slots
        base = (ids[k] * QUADS + quad) * per_quad
        place = place + (row == base + within).astype(jnp.float32)
        sent = jnp.where(row == base + slots, gate, 0.0).astype(jnp.bfloat16)
        gate_block = gate_block + compare_dot(sent, (column == within).astype(jnp.bfloat16))
        position_ref[k : k + 1, :] = ids[k] * capacity + slot
        gates_ref[k : k + 1, :] = gate
    packed = jnp.dot(
        place.astype(jnp.bfloat16), upstream_ref[...], preferred_element_type=jnp.float32
    )
    packed_ref[:, :128] = (packed[:, :128] + gate_block).astype(jnp.bfloat16)
    packed_ref[:, 128:] = packed[:, 128:].astype(jnp.bfloat16)


def pack(ids, logits, upstream, slots):
    tokens, cols = upstream.shape
    rows = EXPERTS * QUADS * (slots + 1)
    return pl.pallas_call(
        pack_kernel,
        out_shape=(
            jax.ShapeDtypeStruct((rows, cols), jnp.bfloat16),
            jax.ShapeDtypeStruct((TOP, tokens), jnp.int32),
            jax.ShapeDtypeStruct((TOP, tokens), jnp.float32),
        ),
        compiler_params=pltpu.CompilerParams(vmem_limit_bytes=VMEM_LIMIT),
        cost_estimate=pl.CostEstimate(
            flops=2 * rows * tokens * cols, bytes_accessed=2 * (rows + tokens) * cols, transcendentals=0
        ),
    )(ids, logits, upstream)


def gather_rows(pieces, j, full_ref):
    part = pieces[0].shape[1]
    for i, piece in enumerate(pieces):
        full_ref[i * part : (i + 1) * part, :] = piece[j]


def first_kernel(p0, p1, p2, p3, weight_ref, hidden_t_ref, proj_ref, product_ref, full_ref):
    for j in range(weight_ref.shape[0]):
        gather_rows((p0, p1, p2, p3), j, full_ref)
        part = compare_dot(full_ref[...], weight_ref[j])
        if j == 0:
            proj_ref[...] = part
        else:
            proj_ref[...] += part
        product_ref[j] = jnp.dot(
            hidden_t_ref[...], full_ref[...], preferred_element_type=jnp.float32
        ).astype(jnp.bfloat16)


def last_kernel(
    quad_ref, p0, p1, p2, p3, weight_ref, hidden_t_ref, proj_ref, hidden_ref, gate_ref,
    grad_ref, partial_ref, product_ref, full_ref, total_ref,
):
    blocks = weight_ref.shape[0]
    for j in range(blocks):
        gather_rows((p0, p1, p2, p3), j, full_ref)
        part = compare_dot(full_ref[...], weight_ref[j])
        if j == 0:
            total_ref[...] = proj_ref[...] + part
        else:
            total_ref[...] += part
        product_ref[j] = jnp.dot(
            hidden_t_ref[...], full_ref[...], preferred_element_type=jnp.float32
        ).astype(jnp.bfloat16)
    rows = p0.shape[1]
    quad = quad_ref[0]
    for i in range(QUADS):
        owner = jnp.bitwise_xor(quad, i)
        proj = total_ref[i * rows : (i + 1) * rows, :]
        partial_ref[owner] = jnp.sum(hidden_ref[i].astype(jnp.float32) * proj, axis=1, keepdims=True)
        grad_ref[owner] = (gate_ref[i] * proj).astype(jnp.bfloat16)


def local(upstream, router_logits, expert_ids, hidden_saved, down_weight):
    tokens, cols = upstream.shape
    tensor_count = lax.axis_size("tp")
    context_count = lax.axis_size("ctx")
    data_count = lax.axis_size("dp")
    capacity = hidden_saved.shape[0] // context_count
    slots = capacity // QUADS
    units = hidden_saved.shape[1]
    rows = context_count * slots
    half = cols // 2
    quad = lax.rem(lax.axis_index("ctx"), QUADS)

    packed, position, gates = pack(expert_ids.T, router_logits.T, upstream, slots)
    outgoing = packed.reshape(context_count, (slots + 1) * cols // 128, 128)
    received = lax.all_to_all(outgoing, "ctx", split_axis=0, concat_axis=0, tiled=True)
    received = received.reshape(context_count, slots + 1, cols)
    own_rows = received[:, :slots].reshape(rows, cols)
    own_gate = received[:, slots, :slots].reshape(rows)

    def swap(x, bit):
        return lax.ppermute(x, "ctx", [(c, c ^ bit) for c in range(context_count)])

    def spread(x):
        core = swap(x, 1)
        other = swap(x, 2)
        return x, core, other, swap(other, 1)

    weight = lax.all_gather(down_weight, "dp", axis=0, tiled=False)
    gathered = [
        lax.all_gather(own_rows[:, s : s + half], "tp", axis=0, tiled=False) for s in (0, half)
    ]
    pair_gate = jnp.stack([own_gate, swap(own_gate, 1)])
    gate = jnp.concatenate([pair_gate, swap(pair_gate, 2)])
    gate = gate.astype(jnp.float32)[:, :, None]

    quads = hidden_saved.reshape(context_count, QUADS, slots, units).transpose(1, 0, 2, 3)
    quads = quads.reshape(QUADS, rows, units)
    hidden = jnp.stack(
        [
            lax.dynamic_index_in_dim(quads, jnp.bitwise_xor(quad, i), 0, keepdims=False)
            for i in range(QUADS)
        ]
    )
    hidden_t = (gate * hidden.astype(jnp.float32)).astype(jnp.bfloat16)
    hidden_t = hidden_t.reshape(QUADS * rows, units).T

    total = QUADS * rows
    scratch = pltpu.VMEM((total, half), jnp.bfloat16)
    flops = 4 * total * units * tensor_count * half
    cost = pl.CostEstimate(flops=flops, bytes_accessed=8 << 20, transcendentals=0)
    product_shape = jax.ShapeDtypeStruct((data_count, units, half), jnp.bfloat16)
    pieces = spread(gathered[0])
    proj, product = pl.pallas_call(
        first_kernel,
        out_shape=(jax.ShapeDtypeStruct((total, units), jnp.float32), product_shape),
        scratch_shapes=[scratch],
        compiler_params=pltpu.CompilerParams(vmem_limit_bytes=VMEM_LIMIT),
        cost_estimate=cost,
    )(*pieces, weight[:, :, :half], hidden_t)
    grad_first = lax.psum_scatter(product, "dp", scatter_dimension=0, tiled=False)
    pieces = spread(gathered[1])
    vmem = pl.BlockSpec(memory_space=pltpu.VMEM)
    hidden_grad, partial, product = pl.pallas_call(
        last_kernel,
        out_shape=(
            jax.ShapeDtypeStruct((QUADS, rows, units), jnp.bfloat16),
            jax.ShapeDtypeStruct((QUADS, rows, 1), jnp.float32),
            product_shape,
        ),
        in_specs=[pl.BlockSpec(memory_space=pltpu.SMEM)] + [vmem] * 9,
        scratch_shapes=[scratch, pltpu.VMEM((total, units), jnp.float32)],
        compiler_params=pltpu.CompilerParams(vmem_limit_bytes=VMEM_LIMIT),
        cost_estimate=cost,
    )(quad.astype(jnp.int32).reshape(1), *pieces, weight[:, :, half:], hidden_t, proj, hidden, gate)
    grad_second = lax.psum_scatter(product, "dp", scatter_dimension=0, tiled=False)
    down_grad = jnp.concatenate([grad_first, grad_second], axis=1)

    def canonical(x):
        x = x.reshape(QUADS, context_count, slots, -1).transpose(1, 0, 2, 3)
        return x.reshape(context_count * capacity, -1)

    hidden_grad = canonical(hidden_grad)
    sums = canonical(partial).reshape(context_count, 1, capacity)
    outgoing_sums = jnp.broadcast_to(sums, (context_count, tensor_count, capacity))
    returned = lax.all_to_all(
        outgoing_sums.reshape(context_count * tensor_count, capacity),
        ("ctx", "tp"), split_axis=0, concat_axis=0, tiled=True,
    )
    expert_sums = returned.reshape(EXPERTS, -1, capacity).sum(axis=1)
    route_grad = jnp.take(expert_sums.reshape(-1), position)
    logit_grad = gates * (route_grad - jnp.sum(gates * route_grad, axis=0, keepdims=True))
    return (hidden_grad, down_grad, logit_grad.T)


def solution(mesh):
    in_specs = (
        P(("dp", "ctx"), "tp"),
        P(("dp", "ctx"), None),
        P(("dp", "ctx"), None),
        P("dp", ("ctx", "tp")),
        P(("ctx", "tp"), "dp"),
    )
    out_specs = (P("dp", ("ctx", "tp")), P(("ctx", "tp"), "dp"), P(("dp", "ctx"), None))
    return jax.shard_map(local, mesh=mesh, in_specs=in_specs, out_specs=out_specs, check_vma=False)
```

```python
import functools

import jax
import jax.numpy as jnp
from jax import lax
from jax.experimental import pallas as pl
from jax.experimental.pallas import tpu as pltpu
from jax.sharding import PartitionSpec as P

EXPERTS = 8
TOP = 2
QUADS = 4
VMEM_LIMIT = 56 * 1024 * 1024
CHUNKS = ((0, 384), (384, 384))


def compare_dot(a, b):
    return lax.dot_general(a, b, (((1,), (1,)), ((), ())), preferred_element_type=jnp.float32)


def slab_rows(capacity):
    return (capacity // 8 + 1) * 8


def pack_kernel(capacity, ids_ref, logits_ref, upstream_ref, packed_ref, position_ref, gates_ref):
    tokens = upstream_ref.shape[0]
    rows = packed_ref.shape[0]
    per_expert = rows // EXPERTS
    ids = [ids_ref[k : k + 1, :] for k in range(TOP)]
    expert = lax.broadcasted_iota(jnp.int32, (EXPERTS, tokens), 0)
    chosen = [(expert == ids[k]).astype(jnp.float32) for k in range(TOP)]
    before = (
        lax.broadcasted_iota(jnp.int32, (tokens, tokens), 0)
        < lax.broadcasted_iota(jnp.int32, (tokens, tokens), 1)
    ).astype(jnp.bfloat16)
    earlier = jnp.dot(
        (chosen[0] + chosen[1]).astype(jnp.bfloat16), before, preferred_element_type=jnp.float32
    )
    row = lax.broadcasted_iota(jnp.int32, (rows, tokens), 0)
    column = lax.broadcasted_iota(jnp.int32, (128, tokens), 0)
    place = jnp.zeros((rows, tokens), jnp.float32)
    gate_block = jnp.zeros((rows, 128), jnp.float32)
    for k in range(TOP):
        slot = jnp.sum(earlier * chosen[k], axis=0, keepdims=True).astype(jnp.int32)
        gate = 1.0 / (1.0 + jnp.exp(logits_ref[1 - k : 2 - k, :] - logits_ref[k : k + 1, :]))
        base = ids[k] * per_expert
        place = place + (row == base + slot).astype(jnp.float32)
        sent = jnp.where(row == base + capacity, gate, 0.0).astype(jnp.bfloat16)
        gate_block = gate_block + compare_dot(sent, (column == slot).astype(jnp.bfloat16))
        position_ref[k : k + 1, :] = ids[k] * capacity + slot
        gates_ref[k : k + 1, :] = gate
    packed = jnp.dot(
        place.astype(jnp.bfloat16), upstream_ref[...], preferred_element_type=jnp.float32
    )
    packed_ref[:, :128] = (packed[:, :128] + gate_block).astype(jnp.bfloat16)
    packed_ref[:, 128:] = packed[:, 128:].astype(jnp.bfloat16)


def pack(ids, logits, upstream, capacity):
    tokens, cols = upstream.shape
    rows = EXPERTS * slab_rows(capacity)
    return pl.pallas_call(
        functools.partial(pack_kernel, capacity),
        out_shape=(
            jax.ShapeDtypeStruct((rows, cols), jnp.bfloat16),
            jax.ShapeDtypeStruct((TOP, tokens), jnp.int32),
            jax.ShapeDtypeStruct((TOP, tokens), jnp.float32),
        ),
        compiler_params=pltpu.CompilerParams(vmem_limit_bytes=VMEM_LIMIT),
        cost_estimate=pl.CostEstimate(
            flops=2 * rows * tokens * cols, bytes_accessed=2 * (rows + tokens) * cols, transcendentals=0
        ),
    )(ids, logits, upstream)


def chunk_kernel(start, first, last, quad_ref, *refs):
    refs = list(refs)
    pieces = [refs.pop(0) for _ in range(QUADS)]
    weight_ref, hidden_t_ref = refs.pop(0), refs.pop(0)
    before_ref = None if first else refs.pop(0)
    hidden_ref, gate_ref = (refs.pop(0), refs.pop(0)) if last else (None, None)
    grad_ref, partial_ref = (refs.pop(0), refs.pop(0)) if last else (None, None)
    proj_ref = None if last else refs.pop(0)
    product_ref = refs.pop(0)
    full, side, hidden_t, total, product, sems = refs[:6]
    hidden = refs[6] if last else None
    blocks, _, width = product.shape
    rows = total.shape[0] // QUADS
    copies = []

    def copy(source, target):
        made = pltpu.make_async_copy(source, target, sems.at[len(copies)])
        copies.append(made)
        made.start()
        return made

    def columns(j):
        return slice(j * width, (j + 1) * width)

    sides = [
        copy(weight_ref.at[j, :, start : start + width], side.at[:, columns(j)])
        for j in range(blocks)
    ]
    loads = []
    for i in range(QUADS):
        at = slice(i * rows, (i + 1) * rows)
        loads.append([copy(pieces[i].at[j], full.at[at, columns(j)]) for j in range(blocks)])
        if not first:
            loads[i].append(copy(before_ref.at[at, :], total.at[at, :]))
        if last:
            loads[i].append(copy(hidden_ref.at[i], hidden.at[i]))
    hidden_t_load = copy(hidden_t_ref, hidden_t)
    stores = []
    for made in sides:
        made.wait()
    for i in range(QUADS):
        for made in loads[i]:
            made.wait()
        at = slice(i * rows, (i + 1) * rows)
        proj = compare_dot(full[at, :], side[...])
        if not first:
            proj = total[at, :] + proj
        if last:
            owner = jnp.bitwise_xor(quad_ref[0], i)
            partial_ref[owner] = jnp.sum(
                hidden[i].astype(jnp.float32) * proj, axis=1, keepdims=True
            )
            grad_ref[owner] = (gate_ref[i] * proj).astype(jnp.bfloat16)
        else:
            total[at, :] = proj
            stores.append(copy(total.at[at, :], proj_ref.at[at, :]))
    hidden_t_load.wait()
    for j in range(blocks):
        result = jnp.dot(hidden_t[...], full[:, columns(j)], preferred_element_type=jnp.float32)
        product[j] = result.astype(jnp.bfloat16)
        stores.append(copy(product.at[j], product_ref.at[j]))
    for made in stores:
        made.wait()


def after(x, *others):
    return lax.optimization_barrier((x,) + others)[0]


def local(upstream, router_logits, expert_ids, hidden_saved, down_weight):
    tokens, cols = upstream.shape
    tensor_count = lax.axis_size("tp")
    context_count = lax.axis_size("ctx")
    data_count = lax.axis_size("dp")
    capacity = hidden_saved.shape[0] // context_count
    units = hidden_saved.shape[1]
    rows = EXPERTS * capacity
    total = QUADS * rows
    quad = lax.rem(lax.axis_index("ctx"), QUADS)

    packed, position, gates = pack(expert_ids.T, router_logits.T, upstream, capacity)
    outgoing = packed.reshape(EXPERTS, slab_rows(capacity), cols)
    groups = [[q + QUADS * e for e in range(EXPERTS)] for q in range(QUADS)]
    received = lax.all_to_all(
        outgoing, "ctx", split_axis=0, concat_axis=0, tiled=True, axis_index_groups=groups
    )
    own_rows = received[:, :capacity].reshape(rows, cols)
    own_gate = received[:, capacity, :capacity].reshape(rows)

    def swap(x, bit):
        return lax.ppermute(x, "ctx", [(c, c ^ bit) for c in range(context_count)])

    weight = lax.all_gather(down_weight, "dp", axis=0, tiled=False)
    gathered = [
        lax.all_gather(own_rows[:, s : s + w], "tp", axis=0, tiled=False) for s, w in CHUNKS
    ]
    pair_gate = jnp.stack([own_gate, swap(own_gate, 1)])
    gate = jnp.concatenate([pair_gate, swap(pair_gate, 2)])
    gate = gate.astype(jnp.float32)[:, :, None]
    quads = hidden_saved.reshape(EXPERTS, QUADS, capacity, units).transpose(1, 0, 2, 3)
    quads = quads.reshape(QUADS, rows, units)
    hidden = jnp.stack(
        [
            lax.dynamic_index_in_dim(quads, jnp.bitwise_xor(quad, i), 0, keepdims=False)
            for i in range(QUADS)
        ]
    )
    hidden_t = (gate * hidden.astype(jnp.float32)).astype(jnp.bfloat16)
    hidden_t = hidden_t.reshape(total, units).T

    def run(start, width, pieces, before=None, last=False):
        first = before is None
        product_shape = jax.ShapeDtypeStruct((data_count, units, width), jnp.bfloat16)
        held = pl.BlockSpec(memory_space=pl.ANY)
        vmem = pl.BlockSpec(memory_space=pltpu.VMEM)
        inputs = list(pieces) + [weight, hidden_t] + ([] if first else [before])
        specs = [pl.BlockSpec(memory_space=pltpu.SMEM)] + [held] * len(inputs)
        if last:
            inputs += [hidden, gate]
            specs += [held, vmem]
            outputs = (
                jax.ShapeDtypeStruct((QUADS, rows, units), jnp.bfloat16),
                jax.ShapeDtypeStruct((QUADS, rows, 1), jnp.float32),
                product_shape,
            )
            out_specs = (vmem, vmem, held)
        else:
            outputs = (jax.ShapeDtypeStruct((total, units), jnp.float32), product_shape)
            out_specs = (held, held)
        scratch = [
            pltpu.VMEM((total, data_count * width), jnp.bfloat16),
            pltpu.VMEM((units, data_count * width), jnp.bfloat16),
            pltpu.VMEM((units, total), jnp.bfloat16),
            pltpu.VMEM((total, units), jnp.float32),
            pltpu.VMEM((data_count, units, width), jnp.bfloat16),
            pltpu.SemaphoreType.DMA((1 + data_count * (QUADS + 2) + 3 * QUADS,)),
        ] + ([pltpu.VMEM((QUADS, rows, units), jnp.bfloat16)] if last else [])
        return pl.pallas_call(
            functools.partial(chunk_kernel, start, first, last),
            out_shape=outputs,
            in_specs=specs,
            out_specs=out_specs,
            scratch_shapes=scratch,
            compiler_params=pltpu.CompilerParams(vmem_limit_bytes=VMEM_LIMIT),
            cost_estimate=pl.CostEstimate(
                flops=18 * 10**9 if last else 1 << 20, bytes_accessed=1 << 20, transcendentals=0
            ),
        )(quad.astype(jnp.int32).reshape(1), *inputs)

    proj, grads = None, []
    for n, (start, width) in enumerate(CHUNKS):
        held, other = gathered[n], swap(gathered[n], 2)
        ahead = (hidden_t,) + tuple(gathered[1:]) if n == 0 else (proj,)
        pieces = (held, swap(held, 1), other, swap(after(other, *ahead), 1))
        if n < len(CHUNKS) - 1:
            proj, product = run(start, width, pieces, proj)
        else:
            hidden_grad, partial, product = run(start, width, pieces, proj, True)
        grads.append(lax.psum_scatter(product, "dp", scatter_dimension=0, tiled=False))
    down_grad = jnp.concatenate(grads, axis=1)

    def canonical(x):
        x = x.reshape(QUADS, EXPERTS, capacity, -1).transpose(1, 0, 2, 3)
        return x.reshape(context_count * capacity, -1)

    hidden_grad = canonical(hidden_grad)
    sums = canonical(partial).reshape(context_count, 1, capacity)
    outgoing_sums = jnp.broadcast_to(sums, (context_count, tensor_count, capacity))
    returned = lax.all_to_all(
        outgoing_sums.reshape(context_count * tensor_count, capacity),
        ("ctx", "tp"), split_axis=0, concat_axis=0, tiled=True,
    )
    expert_sums = returned.reshape(EXPERTS, -1, capacity).sum(axis=1)
    route_grad = jnp.take(expert_sums.reshape(-1), position)
    logit_grad = gates * (route_grad - jnp.sum(gates * route_grad, axis=0, keepdims=True))
    return (hidden_grad, down_grad, logit_grad.T)


def solution(mesh):
    in_specs = (
        P(("dp", "ctx"), "tp"),
        P(("dp", "ctx"), None),
        P(("dp", "ctx"), None),
        P("dp", ("ctx", "tp")),
        P(("ctx", "tp"), "dp"),
    )
    out_specs = (P("dp", ("ctx", "tp")), P(("ctx", "tp"), "dp"), P(("dp", "ctx"), None))
    return jax.shard_map(local, mesh=mesh, in_specs=in_specs, out_specs=out_specs, check_vma=False)
```

```python
import functools

import jax
import jax.numpy as jnp
from jax import lax
from jax.experimental import pallas as pl
from jax.experimental.pallas import tpu as pltpu
from jax.sharding import PartitionSpec as P

EXPERTS = 8
TOP = 2
QUADS = 4
VMEM_LIMIT = 56 * 1024 * 1024
CHUNKS = 3
RELATIVE = (1,)
WEIGH = (5 * 10**9, 1 << 20, 10 * 10**9)


def compare_dot(a, b):
    return lax.dot_general(a, b, (((1,), (1,)), ((), ())), preferred_element_type=jnp.float32)


def slab_rows(capacity):
    return (capacity // 8 + 1) * 8


def pack_kernel(capacity, ids_ref, logits_ref, upstream_ref, packed_ref, position_ref, gates_ref):
    tokens = upstream_ref.shape[0]
    rows = packed_ref.shape[0]
    per_expert = rows // EXPERTS
    ids = [ids_ref[k : k + 1, :] for k in range(TOP)]
    expert = lax.broadcasted_iota(jnp.int32, (EXPERTS, tokens), 0)
    chosen = [(expert == ids[k]).astype(jnp.float32) for k in range(TOP)]
    before = (
        lax.broadcasted_iota(jnp.int32, (tokens, tokens), 0)
        < lax.broadcasted_iota(jnp.int32, (tokens, tokens), 1)
    ).astype(jnp.bfloat16)
    earlier = jnp.dot(
        (chosen[0] + chosen[1]).astype(jnp.bfloat16), before, preferred_element_type=jnp.float32
    )
    row = lax.broadcasted_iota(jnp.int32, (rows, tokens), 0)
    column = lax.broadcasted_iota(jnp.int32, (128, tokens), 0)
    place = jnp.zeros((rows, tokens), jnp.float32)
    gate_block = jnp.zeros((rows, 128), jnp.float32)
    for k in range(TOP):
        slot = jnp.sum(earlier * chosen[k], axis=0, keepdims=True).astype(jnp.int32)
        gate = 1.0 / (1.0 + jnp.exp(logits_ref[1 - k : 2 - k, :] - logits_ref[k : k + 1, :]))
        base = ids[k] * per_expert
        place = place + (row == base + slot).astype(jnp.float32)
        sent = jnp.where(row == base + capacity, gate, 0.0).astype(jnp.bfloat16)
        gate_block = gate_block + compare_dot(sent, (column == slot).astype(jnp.bfloat16))
        position_ref[k : k + 1, :] = ids[k] * capacity + slot
        gates_ref[k : k + 1, :] = gate
    packed = jnp.dot(
        place.astype(jnp.bfloat16), upstream_ref[...], preferred_element_type=jnp.float32
    )
    packed_ref[:, :128] = (packed[:, :128] + gate_block).astype(jnp.bfloat16)
    packed_ref[:, 128:] = packed[:, 128:].astype(jnp.bfloat16)


def pack(ids, logits, upstream, capacity):
    tokens, cols = upstream.shape
    rows = EXPERTS * slab_rows(capacity)
    return pl.pallas_call(
        functools.partial(pack_kernel, capacity),
        out_shape=(
            jax.ShapeDtypeStruct((rows, cols), jnp.bfloat16),
            jax.ShapeDtypeStruct((TOP, tokens), jnp.int32),
            jax.ShapeDtypeStruct((TOP, tokens), jnp.float32),
        ),
        compiler_params=pltpu.CompilerParams(vmem_limit_bytes=VMEM_LIMIT),
        cost_estimate=pl.CostEstimate(
            flops=2 * rows * tokens * cols, bytes_accessed=2 * (rows + tokens) * cols, transcendentals=0
        ),
    )(ids, logits, upstream)


class Copies:
    def __init__(self, sems):
        self.sems, self.count = sems, 0

    def __call__(self, source, target):
        made = pltpu.make_async_copy(source, target, self.sems.at[self.count])
        self.count += 1
        made.start()
        return made


def spans(size, count):
    return [slice(i * size, (i + 1) * size) for i in range(count)]


def load_pieces(copy, pieces, full):
    rows, blocks = full.shape[0] // QUADS, pieces[0].shape[0]
    width = full.shape[1] // blocks
    return [
        [
            copy(pieces[i].at[j], full.at[at, column])
            for j, column in enumerate(spans(width, blocks))
        ]
        for i, at in enumerate(spans(rows, QUADS))
    ]


def wait(copies):
    for made in copies:
        made.wait()


def write_product(copy, relative, place_ref, hidden_t, full, product, product_ref):
    blocks, _, width = product.shape
    stores = []
    for j, column in enumerate(spans(width, blocks)):
        result = jnp.dot(hidden_t[...], full[:, column], preferred_element_type=jnp.float32)
        product[j] = result.astype(jnp.bfloat16)
        place = lax.rem(place_ref[1] + blocks - j, blocks) if relative else j
        stores.append(copy(product.at[j], product_ref.at[place]))
    return stores


def both_kernel(
    start, first, relative, place_ref, p0, p1, p2, p3, weight_ref, hidden_t_ref, before_ref,
    proj_ref, product_ref, full, side, hidden_t, total, product, sems,
):
    copy = Copies(sems)
    blocks, _, width = product.shape
    rows = total.shape[0] // QUADS
    sides = [
        copy(weight_ref.at[j, :, start : start + width], side.at[:, column])
        for j, column in enumerate(spans(width, blocks))
    ]
    loads = load_pieces(copy, (p0, p1, p2, p3), full)
    if not first:
        for i, at in enumerate(spans(rows, QUADS)):
            loads[i].append(copy(before_ref.at[at, :], total.at[at, :]))
    hidden_t_load = copy(hidden_t_ref, hidden_t)
    stores = []
    wait(sides)
    for i, at in enumerate(spans(rows, QUADS)):
        wait(loads[i])
        proj = compare_dot(full[at, :], side[...])
        total[at, :] = proj if first else total[at, :] + proj
        stores.append(copy(total.at[at, :], proj_ref.at[at, :]))
    hidden_t_load.wait()
    stores += write_product(copy, relative, place_ref, hidden_t, full, product, product_ref)
    wait(stores)


def product_kernel(
    relative, place_ref, p0, p1, p2, p3, hidden_t_ref, product_ref, full, hidden_t, product, sems
):
    copy = Copies(sems)
    hidden_t_load = copy(hidden_t_ref, hidden_t)
    for loads in load_pieces(copy, (p0, p1, p2, p3), full):
        wait(loads)
    hidden_t_load.wait()
    wait(write_product(copy, relative, place_ref, hidden_t, full, product, product_ref))


def last_kernel(
    start, place_ref, p0, p1, p2, p3, weight_ref, before_ref, hidden_ref, gate_ref,
    grad_ref, partial_ref, full, side, total, hidden, grad, sems,
):
    copy = Copies(sems)
    blocks = p0.shape[0]
    width = full.shape[1] // blocks
    rows = total.shape[0] // QUADS
    sides = [
        copy(weight_ref.at[j, :, start : start + width], side.at[:, column])
        for j, column in enumerate(spans(width, blocks))
    ]
    loads = load_pieces(copy, (p0, p1, p2, p3), full)
    for i, at in enumerate(spans(rows, QUADS)):
        loads[i].append(copy(before_ref.at[at, :], total.at[at, :]))
        loads[i].append(copy(hidden_ref.at[i], hidden.at[i]))
    wait(sides)
    stores = []
    for i, at in enumerate(spans(rows, QUADS)):
        wait(loads[i])
        proj = total[at, :] + compare_dot(full[at, :], side[...])
        owner = jnp.bitwise_xor(place_ref[0], i)
        partial_ref[owner] = jnp.sum(hidden[i].astype(jnp.float32) * proj, axis=1, keepdims=True)
        grad[i] = (gate_ref[i] * proj).astype(jnp.bfloat16)
        stores.append(copy(grad.at[i], grad_ref.at[owner]))
    wait(stores)


def after(x, *others):
    return lax.optimization_barrier((x,) + others)[0]


def local(upstream, router_logits, expert_ids, hidden_saved, down_weight):
    tokens, cols = upstream.shape
    tensor_count = lax.axis_size("tp")
    context_count = lax.axis_size("ctx")
    data_count = lax.axis_size("dp")
    capacity = hidden_saved.shape[0] // context_count
    units = hidden_saved.shape[1]
    rows = EXPERTS * capacity
    total = QUADS * rows
    quad = lax.rem(lax.axis_index("ctx"), QUADS)

    packed, position, gates = pack(expert_ids.T, router_logits.T, upstream, capacity)
    outgoing = packed.reshape(EXPERTS, slab_rows(capacity), cols)
    groups = [[q + QUADS * e for e in range(EXPERTS)] for q in range(QUADS)]
    received = lax.all_to_all(
        outgoing, "ctx", split_axis=0, concat_axis=0, tiled=True, axis_index_groups=groups
    )
    own_rows = received[:, :capacity].reshape(rows, cols)
    own_gate = received[:, capacity, :capacity].reshape(rows)

    def swap(x, bit):
        return lax.ppermute(x, "ctx", [(c, c ^ bit) for c in range(context_count)])

    quads = hidden_saved.reshape(EXPERTS, QUADS, capacity, units).transpose(1, 0, 2, 3)
    quads = quads.reshape(QUADS, rows, units)
    hidden = jnp.stack(
        [
            lax.dynamic_index_in_dim(quads, jnp.bitwise_xor(quad, i), 0, keepdims=False)
            for i in range(QUADS)
        ]
    )

    weight = lax.all_gather(down_weight, "dp", axis=0, tiled=False)
    width = cols // CHUNKS
    gathered = [
        lax.all_gather(own_rows[:, column], "tp", axis=0, tiled=False)
        for column in spans(width, CHUNKS)
    ]

    pair_gate = jnp.stack([own_gate, swap(own_gate, 1)])
    gate = jnp.concatenate([pair_gate, swap(pair_gate, 2)])
    gate = gate.astype(jnp.float32)[:, :, None]
    hidden_t = (gate * hidden.astype(jnp.float32)).astype(jnp.bfloat16)
    hidden_t = hidden_t.reshape(total, units).T

    place = jnp.stack([quad, lax.axis_index("dp")]).astype(jnp.int32)
    held = pl.BlockSpec(memory_space=pl.ANY)
    vmem = pl.BlockSpec(memory_space=pltpu.VMEM)
    smem = pl.BlockSpec(memory_space=pltpu.SMEM)
    product_shape = jax.ShapeDtypeStruct((data_count, units, width), jnp.bfloat16)
    full = pltpu.VMEM((total, data_count * width), jnp.bfloat16)
    side = pltpu.VMEM((units, data_count * width), jnp.bfloat16)
    hidden_t_space = pltpu.VMEM((units, total), jnp.bfloat16)
    total_space = pltpu.VMEM((total, units), jnp.float32)
    product_space = pltpu.VMEM((data_count, units, width), jnp.bfloat16)
    quad_space = pltpu.VMEM((QUADS, rows, units), jnp.bfloat16)
    sems = pltpu.SemaphoreType.DMA((data_count * (QUADS + 2) + 3 * QUADS + 1,))

    def call(kernel, inputs, specs, outputs, out_specs, scratch, weigh):
        return pl.pallas_call(
            kernel,
            out_shape=outputs,
            in_specs=specs,
            out_specs=out_specs,
            scratch_shapes=scratch,
            compiler_params=pltpu.CompilerParams(vmem_limit_bytes=VMEM_LIMIT),
            cost_estimate=pl.CostEstimate(
                flops=weigh, bytes_accessed=1 << 20, transcendentals=0
            ),
        )(place, *inputs)

    def turn(x, k):
        return lax.ppermute(x, "dp", [(d, (d + k) % data_count) for d in range(data_count)])

    def settle(relative, product):
        if not relative:
            return lax.psum_scatter(product, "dp", scatter_dimension=0, tiled=False)
        grad = product[0].astype(jnp.float32)
        for k in (2, 1, 3):
            grad = grad + turn(product[k], data_count - k).astype(jnp.float32)
        return grad.astype(jnp.bfloat16)

    core = [swap(x, 1) for x in gathered]
    others = [swap(x, 2) for x in gathered]
    proj, grads = None, []
    for n in range(CHUNKS):
        first, last = n == 0, n == CHUNKS - 1
        relative = n in RELATIVE
        other = others[n]
        ahead = (proj,) if last else (hidden_t, others[1], *gathered)
        pieces = (gathered[n], core[n], other, swap(after(other, *ahead), 1))
        if last:
            product = call(
                functools.partial(product_kernel, relative),
                pieces + (hidden_t,), [smem] + [held] * 5, product_shape, held,
                [full, hidden_t_space, product_space, sems], WEIGH[n],
            )
            hidden_grad, partial = call(
                functools.partial(last_kernel, n * width),
                pieces + (weight, proj, after(hidden, product), gate),
                [smem] + [held] * 7 + [vmem],
                (
                    jax.ShapeDtypeStruct((QUADS, rows, units), jnp.bfloat16),
                    jax.ShapeDtypeStruct((QUADS, rows, 1), jnp.float32),
                ),
                (held, vmem), [full, side, total_space, quad_space, quad_space, sems], 1 << 20,
            )
        else:
            proj, product = call(
                functools.partial(both_kernel, n * width, first, relative),
                pieces + (weight, hidden_t, hidden_t if first else proj),
                [smem] + [held] * 7,
                (jax.ShapeDtypeStruct((total, units), jnp.float32), product_shape), (held, held),
                [full, side, hidden_t_space, total_space, product_space, sems], WEIGH[n],
            )
        grads.append(settle(relative, product))
    down_grad = jnp.concatenate(grads, axis=1)

    def canonical(x):
        x = x.reshape(QUADS, EXPERTS, capacity, -1).transpose(1, 0, 2, 3)
        return x.reshape(context_count * capacity, -1)

    hidden_grad = canonical(hidden_grad)
    sums = canonical(partial).reshape(context_count, 1, capacity)
    outgoing_sums = jnp.broadcast_to(sums, (context_count, tensor_count, capacity))
    returned = lax.all_to_all(
        outgoing_sums.reshape(context_count * tensor_count, capacity),
        ("ctx", "tp"), split_axis=0, concat_axis=0, tiled=True,
    )
    expert_sums = returned.reshape(EXPERTS, -1, capacity).sum(axis=1)
    route_grad = jnp.take(expert_sums.reshape(-1), position)
    logit_grad = gates * (route_grad - jnp.sum(gates * route_grad, axis=0, keepdims=True))
    return (hidden_grad, down_grad, logit_grad.T)


def solution(mesh):
    in_specs = (
        P(("dp", "ctx"), "tp"),
        P(("dp", "ctx"), None),
        P(("dp", "ctx"), None),
        P("dp", ("ctx", "tp")),
        P(("ctx", "tp"), "dp"),
    )
    out_specs = (P("dp", ("ctx", "tp")), P(("ctx", "tp"), "dp"), P(("dp", "ctx"), None))
    return jax.shard_map(local, mesh=mesh, in_specs=in_specs, out_specs=out_specs, check_vma=False)
```

```python
import functools

import jax
import jax.numpy as jnp
from jax import lax
from jax.experimental import pallas as pl
from jax.experimental.pallas import tpu as pltpu
from jax.sharding import PartitionSpec as P

EXPERTS = 8
TOP = 2
QUADS = 4
VMEM_LIMIT = 56 * 1024 * 1024
CHUNKS = 2
RELATIVE = ()
WEIGH = (1 << 20, 18 * 10**9)


def compare_dot(a, b):
    return lax.dot_general(a, b, (((1,), (1,)), ((), ())), preferred_element_type=jnp.float32)


def slab_rows(capacity):
    return (capacity // 8 + 1) * 8


def pack_kernel(capacity, ids_ref, logits_ref, upstream_ref, packed_ref, position_ref, gates_ref):
    tokens = upstream_ref.shape[0]
    rows = packed_ref.shape[0]
    per_expert = rows // EXPERTS
    ids = [ids_ref[k : k + 1, :] for k in range(TOP)]
    expert = lax.broadcasted_iota(jnp.int32, (EXPERTS, tokens), 0)
    chosen = [(expert == ids[k]).astype(jnp.float32) for k in range(TOP)]
    before = (
        lax.broadcasted_iota(jnp.int32, (tokens, tokens), 0)
        < lax.broadcasted_iota(jnp.int32, (tokens, tokens), 1)
    ).astype(jnp.bfloat16)
    earlier = jnp.dot(
        (chosen[0] + chosen[1]).astype(jnp.bfloat16), before, preferred_element_type=jnp.float32
    )
    row = lax.broadcasted_iota(jnp.int32, (rows, tokens), 0)
    column = lax.broadcasted_iota(jnp.int32, (128, tokens), 0)
    place = jnp.zeros((rows, tokens), jnp.float32)
    gate_block = jnp.zeros((rows, 128), jnp.float32)
    for k in range(TOP):
        slot = jnp.sum(earlier * chosen[k], axis=0, keepdims=True).astype(jnp.int32)
        gate = 1.0 / (1.0 + jnp.exp(logits_ref[1 - k : 2 - k, :] - logits_ref[k : k + 1, :]))
        base = ids[k] * per_expert
        place = place + (row == base + slot).astype(jnp.float32)
        sent = jnp.where(row == base + capacity, gate, 0.0).astype(jnp.bfloat16)
        gate_block = gate_block + compare_dot(sent, (column == slot).astype(jnp.bfloat16))
        position_ref[k : k + 1, :] = ids[k] * capacity + slot
        gates_ref[k : k + 1, :] = gate
    packed = jnp.dot(
        place.astype(jnp.bfloat16), upstream_ref[...], preferred_element_type=jnp.float32
    )
    packed_ref[:, :128] = (packed[:, :128] + gate_block).astype(jnp.bfloat16)
    packed_ref[:, 128:] = packed[:, 128:].astype(jnp.bfloat16)


def pack(ids, logits, upstream, capacity):
    tokens, cols = upstream.shape
    rows = EXPERTS * slab_rows(capacity)
    return pl.pallas_call(
        functools.partial(pack_kernel, capacity),
        out_shape=(
            jax.ShapeDtypeStruct((rows, cols), jnp.bfloat16),
            jax.ShapeDtypeStruct((TOP, tokens), jnp.int32),
            jax.ShapeDtypeStruct((TOP, tokens), jnp.float32),
        ),
        compiler_params=pltpu.CompilerParams(vmem_limit_bytes=VMEM_LIMIT),
        cost_estimate=pl.CostEstimate(
            flops=2 * rows * tokens * cols, bytes_accessed=2 * (rows + tokens) * cols, transcendentals=0
        ),
    )(ids, logits, upstream)


class Copies:
    def __init__(self, sems):
        self.sems, self.count = sems, 0

    def __call__(self, source, target):
        made = pltpu.make_async_copy(source, target, self.sems.at[self.count])
        self.count += 1
        made.start()
        return made


def spans(size, count):
    return [slice(i * size, (i + 1) * size) for i in range(count)]


def load_pieces(copy, pieces, full):
    rows, blocks = full.shape[0] // QUADS, pieces[0].shape[0]
    width = full.shape[1] // blocks
    return [
        [
            copy(pieces[i].at[j, 0:rows, :], full.at[at, column])
            for j, column in enumerate(spans(width, blocks))
        ]
        for i, at in enumerate(spans(rows, QUADS))
    ]


def wait(copies):
    for made in copies:
        made.wait()


def write_product(copy, relative, place_ref, hidden_t, full, product, product_ref):
    blocks, _, width = product.shape
    stores = []
    for j, column in enumerate(spans(width, blocks)):
        result = jnp.dot(hidden_t[...], full[:, column], preferred_element_type=jnp.float32)
        product[j] = result.astype(jnp.bfloat16)
        place = lax.rem(place_ref[1] + blocks - j, blocks) if relative else j
        stores.append(copy(product.at[j], product_ref.at[place]))
    return stores


def both_kernel(
    start, first, relative, place_ref, p0, p1, p2, p3, weight_ref, hidden_t_ref, before_ref,
    proj_ref, product_ref, full, side, hidden_t, total, product, sems,
):
    copy = Copies(sems)
    blocks, _, width = product.shape
    rows = total.shape[0] // QUADS
    sides = [
        copy(weight_ref.at[j, :, start : start + width], side.at[:, column])
        for j, column in enumerate(spans(width, blocks))
    ]
    loads = load_pieces(copy, (p0, p1, p2, p3), full)
    if not first:
        for i, at in enumerate(spans(rows, QUADS)):
            loads[i].append(copy(before_ref.at[at, :], total.at[at, :]))
    hidden_t_load = copy(hidden_t_ref, hidden_t)
    stores = []
    wait(sides)
    for i, at in enumerate(spans(rows, QUADS)):
        wait(loads[i])
        proj = compare_dot(full[at, :], side[...])
        total[at, :] = proj if first else total[at, :] + proj
        stores.append(copy(total.at[at, :], proj_ref.at[at, :]))
    hidden_t_load.wait()
    stores += write_product(copy, relative, place_ref, hidden_t, full, product, product_ref)
    wait(stores)


def product_kernel(
    relative, place_ref, p0, p1, p2, p3, hidden_t_ref, product_ref, full, hidden_t, product, sems
):
    copy = Copies(sems)
    hidden_t_load = copy(hidden_t_ref, hidden_t)
    for loads in load_pieces(copy, (p0, p1, p2, p3), full):
        wait(loads)
    hidden_t_load.wait()
    wait(write_product(copy, relative, place_ref, hidden_t, full, product, product_ref))


def last_kernel(
    start, place_ref, p0, p1, p2, p3, weight_ref, before_ref, hidden_ref, gate_ref,
    grad_ref, partial_ref, full, side, total, hidden, grad, sems,
):
    copy = Copies(sems)
    blocks = p0.shape[0]
    width = full.shape[1] // blocks
    rows = total.shape[0] // QUADS
    sides = [
        copy(weight_ref.at[j, :, start : start + width], side.at[:, column])
        for j, column in enumerate(spans(width, blocks))
    ]
    loads = load_pieces(copy, (p0, p1, p2, p3), full)
    for i, at in enumerate(spans(rows, QUADS)):
        loads[i].append(copy(before_ref.at[at, :], total.at[at, :]))
        loads[i].append(copy(hidden_ref.at[i], hidden.at[i]))
    ones = jnp.ones((8, hidden.shape[2]), jnp.float32)
    wait(sides)
    stores = []
    for i, at in enumerate(spans(rows, QUADS)):
        wait(loads[i])
        proj = total[at, :] + compare_dot(full[at, :], side[...])
        owner = jnp.bitwise_xor(place_ref[0], i)
        partial_ref[owner] = lax.dot_general(
            ones, hidden[i].astype(jnp.float32) * proj, (((1,), (1,)), ((), ())),
            precision=lax.Precision.HIGHEST, preferred_element_type=jnp.float32,
        )
        grad[i] = (gate_ref[i] * proj).astype(jnp.bfloat16)
        stores.append(copy(grad.at[i], grad_ref.at[owner]))
    wait(stores)


def after(x, *others):
    return lax.optimization_barrier((x,) + others)[0]


def local(upstream, router_logits, expert_ids, hidden_saved, down_weight):
    tokens, cols = upstream.shape
    tensor_count = lax.axis_size("tp")
    context_count = lax.axis_size("ctx")
    data_count = lax.axis_size("dp")
    capacity = hidden_saved.shape[0] // context_count
    units = hidden_saved.shape[1]
    rows = EXPERTS * capacity
    total = QUADS * rows
    quad = lax.rem(lax.axis_index("ctx"), QUADS)

    packed, position, gates = pack(expert_ids.T, router_logits.T, upstream, capacity)
    outgoing = packed.reshape(EXPERTS, slab_rows(capacity), cols)
    groups = [[q + QUADS * e for e in range(EXPERTS)] for q in range(QUADS)]
    received = lax.all_to_all(
        outgoing, "ctx", split_axis=0, concat_axis=0, tiled=True, axis_index_groups=groups
    )
    own_rows = received[:, :capacity].reshape(rows, cols)
    gate_line = received[:, capacity, :capacity].reshape(1, rows)

    def swap(x, bit):
        return lax.ppermute(x, "ctx", [(c, c ^ bit) for c in range(context_count)])

    quads = hidden_saved.reshape(EXPERTS, QUADS, capacity, units).transpose(1, 0, 2, 3)
    quads = quads.reshape(QUADS, rows, units)
    hidden = jnp.stack(
        [
            lax.dynamic_index_in_dim(quads, jnp.bitwise_xor(quad, i), 0, keepdims=False)
            for i in range(QUADS)
        ]
    )

    hidden_turned = hidden.reshape(total, units).T
    weight = lax.all_gather(down_weight, "dp", axis=0, tiled=False)
    width = cols // CHUNKS
    sent = [own_rows[:, column] for column in spans(width, CHUNKS)]
    sent[0] = jnp.concatenate([sent[0], jnp.pad(gate_line, ((0, 7), (0, width - rows)))])
    sent[0] = after(sent[0], hidden, hidden_turned)
    gathered = [lax.all_gather(x, "tp", axis=0, tiled=False) for x in sent]
    others = [swap(x, 2) for x in gathered]
    core = [swap(after(x, others[0], *gathered), 1) for x in gathered]
    last_others = swap(after(others[0], *gathered), 1)
    firsts = (gathered[0], core[0], others[0], last_others)

    gate = jnp.stack([piece[0, rows, :rows] for piece in firsts]).astype(jnp.float32)
    hidden_t = (hidden_turned.astype(jnp.float32) * gate.reshape(1, total)).astype(jnp.bfloat16)
    gate_column = gate[:, :, None]

    place = jnp.stack([quad, lax.axis_index("dp")]).astype(jnp.int32)
    held = pl.BlockSpec(memory_space=pl.ANY)
    vmem = pl.BlockSpec(memory_space=pltpu.VMEM)
    smem = pl.BlockSpec(memory_space=pltpu.SMEM)
    product_shape = jax.ShapeDtypeStruct((data_count, units, width), jnp.bfloat16)
    full = pltpu.VMEM((total, data_count * width), jnp.bfloat16)
    side = pltpu.VMEM((units, data_count * width), jnp.bfloat16)
    hidden_t_space = pltpu.VMEM((units, total), jnp.bfloat16)
    total_space = pltpu.VMEM((total, units), jnp.float32)
    product_space = pltpu.VMEM((data_count, units, width), jnp.bfloat16)
    quad_space = pltpu.VMEM((QUADS, rows, units), jnp.bfloat16)
    sems = pltpu.SemaphoreType.DMA((data_count * (QUADS + 2) + 3 * QUADS + 1,))

    def call(kernel, inputs, specs, outputs, out_specs, scratch, weigh, place=place):
        return pl.pallas_call(
            kernel,
            out_shape=outputs,
            in_specs=specs,
            out_specs=out_specs,
            scratch_shapes=scratch,
            compiler_params=pltpu.CompilerParams(vmem_limit_bytes=VMEM_LIMIT),
            cost_estimate=pl.CostEstimate(
                flops=weigh, bytes_accessed=1 << 20, transcendentals=0
            ),
        )(place, *inputs)

    def turn(x, k):
        return lax.ppermute(x, "dp", [(d, (d + k) % data_count) for d in range(data_count)])

    def settle(relative, product):
        if not relative:
            return lax.psum_scatter(product, "dp", scatter_dimension=0, tiled=False)
        grad = product[0].astype(jnp.float32)
        for k in (2, 1, 3):
            grad = grad + turn(product[k], data_count - k).astype(jnp.float32)
        return grad.astype(jnp.bfloat16)

    proj, grads = None, []
    for n in range(CHUNKS):
        first, last = n == 0, n == CHUNKS - 1
        relative = n in RELATIVE
        if first:
            pieces = firsts
        else:
            pieces = (gathered[n], core[n], others[n], swap(after(others[n], proj, gate_column), 1))
        if last:
            product = call(
                functools.partial(product_kernel, relative),
                pieces + (hidden_t,), [smem] + [held] * 5, product_shape, held,
                [full, hidden_t_space, product_space, sems], WEIGH[n],
            )
            hidden_grad, partial = call(
                functools.partial(last_kernel, n * width),
                pieces + (weight, proj, hidden, gate_column),
                [smem] + [held] * 7 + [vmem],
                (
                    jax.ShapeDtypeStruct((QUADS, rows, units), jnp.bfloat16),
                    jax.ShapeDtypeStruct((QUADS, 8, rows), jnp.float32),
                ),
                (held, vmem), [full, side, total_space, quad_space, quad_space, sems], 1 << 20,
                after(place, product),
            )
        else:
            proj, product = call(
                functools.partial(both_kernel, n * width, first, relative),
                pieces + (weight, hidden_t, hidden_t if first else proj),
                [smem] + [held] * 7,
                (jax.ShapeDtypeStruct((total, units), jnp.float32), product_shape), (held, held),
                [full, side, hidden_t_space, total_space, product_space, sems], WEIGH[n],
            )
        grads.append(settle(relative, product))
    down_grad = jnp.concatenate(grads, axis=1)

    def canonical(x):
        x = x.reshape(QUADS, EXPERTS, capacity, -1).transpose(1, 0, 2, 3)
        return x.reshape(context_count * capacity, -1)

    hidden_grad = canonical(hidden_grad)
    sums = partial[:, 0].reshape(QUADS, EXPERTS, capacity).transpose(1, 0, 2)
    sums = sums.reshape(context_count, 1, capacity)
    outgoing_sums = jnp.broadcast_to(sums, (context_count, tensor_count, capacity))
    returned = lax.all_to_all(
        outgoing_sums.reshape(context_count * tensor_count, capacity),
        ("ctx", "tp"), split_axis=0, concat_axis=0, tiled=True,
    )
    expert_sums = returned.reshape(EXPERTS, -1, capacity).sum(axis=1)
    route_grad = jnp.take(expert_sums.reshape(-1), position)
    logit_grad = gates * (route_grad - jnp.sum(gates * route_grad, axis=0, keepdims=True))
    return (hidden_grad, down_grad, logit_grad.T)


def solution(mesh):
    in_specs = (
        P(("dp", "ctx"), "tp"),
        P(("dp", "ctx"), None),
        P(("dp", "ctx"), None),
        P("dp", ("ctx", "tp")),
        P(("ctx", "tp"), "dp"),
    )
    out_specs = (P("dp", ("ctx", "tp")), P(("ctx", "tp"), "dp"), P(("dp", "ctx"), None))
    return jax.shard_map(local, mesh=mesh, in_specs=in_specs, out_specs=out_specs, check_vma=False)
```

```python
import functools

import jax
import jax.numpy as jnp
from jax import lax
from jax.experimental import pallas as pl
from jax.experimental.pallas import tpu as pltpu
from jax.sharding import PartitionSpec as P

EXPERTS = 8
TOP = 2
QUADS = 4
VMEM_LIMIT = 56 * 1024 * 1024
CHUNKS = 2
WEIGH = (1 << 20, 1 << 20, 18 * 10**9)


def compare_dot(a, b):
    return lax.dot_general(a, b, (((1,), (1,)), ((), ())), preferred_element_type=jnp.float32)


def slab_rows(capacity):
    return (capacity // 8 + 1) * 8


def pack_kernel(capacity, ids_ref, logits_ref, upstream_ref, packed_ref, position_ref, gates_ref):
    tokens = upstream_ref.shape[0]
    rows = packed_ref.shape[0]
    per_expert = rows // EXPERTS
    ids = [ids_ref[k : k + 1, :] for k in range(TOP)]
    expert = lax.broadcasted_iota(jnp.int32, (EXPERTS, tokens), 0)
    chosen = [(expert == ids[k]).astype(jnp.float32) for k in range(TOP)]
    before = (
        lax.broadcasted_iota(jnp.int32, (tokens, tokens), 0)
        < lax.broadcasted_iota(jnp.int32, (tokens, tokens), 1)
    ).astype(jnp.bfloat16)
    earlier = jnp.dot(
        (chosen[0] + chosen[1]).astype(jnp.bfloat16), before, preferred_element_type=jnp.float32
    )
    row = lax.broadcasted_iota(jnp.int32, (rows, tokens), 0)
    column = lax.broadcasted_iota(jnp.int32, (128, tokens), 0)
    place = jnp.zeros((rows, tokens), jnp.float32)
    gate_block = jnp.zeros((rows, 128), jnp.float32)
    for k in range(TOP):
        slot = jnp.sum(earlier * chosen[k], axis=0, keepdims=True).astype(jnp.int32)
        gate = 1.0 / (1.0 + jnp.exp(logits_ref[1 - k : 2 - k, :] - logits_ref[k : k + 1, :]))
        base = ids[k] * per_expert
        place = place + (row == base + slot).astype(jnp.float32)
        sent = jnp.where(row == base + capacity, gate, 0.0).astype(jnp.bfloat16)
        gate_block = gate_block + compare_dot(sent, (column == slot).astype(jnp.bfloat16))
        position_ref[k : k + 1, :] = ids[k] * capacity + slot
        gates_ref[k : k + 1, :] = gate
    packed = jnp.dot(
        place.astype(jnp.bfloat16), upstream_ref[...], preferred_element_type=jnp.float32
    )
    packed_ref[:, :128] = (packed[:, :128] + gate_block).astype(jnp.bfloat16)
    packed_ref[:, 128:] = packed[:, 128:].astype(jnp.bfloat16)


def pack(ids, logits, upstream, capacity):
    tokens, cols = upstream.shape
    rows = EXPERTS * slab_rows(capacity)
    return pl.pallas_call(
        functools.partial(pack_kernel, capacity),
        out_shape=(
            jax.ShapeDtypeStruct((rows, cols), jnp.bfloat16),
            jax.ShapeDtypeStruct((TOP, tokens), jnp.int32),
            jax.ShapeDtypeStruct((TOP, tokens), jnp.float32),
        ),
        compiler_params=pltpu.CompilerParams(vmem_limit_bytes=VMEM_LIMIT),
        cost_estimate=pl.CostEstimate(
            flops=2 * rows * tokens * cols, bytes_accessed=2 * (rows + tokens) * cols, transcendentals=0
        ),
    )(ids, logits, upstream)


class Copies:
    def __init__(self, sems):
        self.sems, self.count = sems, 0

    def __call__(self, source, target):
        made = pltpu.make_async_copy(source, target, self.sems.at[self.count])
        self.count += 1
        made.start()
        return made


def spans(size, count):
    return [slice(i * size, (i + 1) * size) for i in range(count)]


def wait(copies):
    for made in copies:
        made.wait()


def load_rows(copy, pieces, full):
    rows, blocks = full.shape[0] // len(pieces), pieces[0].shape[0]
    columns = spans(full.shape[1] // blocks, blocks)
    return [
        [copy(piece.at[j, 0:rows, :], full.at[at, column]) for j, column in enumerate(columns)]
        for piece, at in zip(pieces, spans(rows, len(pieces)))
    ]


def load_weight(copy, weight_ref, start, side):
    blocks = weight_ref.shape[0]
    width = side.shape[1] // blocks
    return [
        copy(weight_ref.at[j, :, start : start + width], side.at[:, column])
        for j, column in enumerate(spans(width, blocks))
    ]


def product_kernel(p0, p1, p2, p3, hidden_t_ref, product_ref, full, hidden_t, product, sems):
    copy = Copies(sems)
    blocks, _, width = product.shape
    rows = full.shape[0] // QUADS
    columns = spans(width, blocks)
    first = [copy(hidden_t_ref, hidden_t)]
    loads = [
        [
            copy(piece.at[j, 0:rows, :], full.at[at, column])
            for piece, at in zip((p0, p1, p2, p3), spans(rows, QUADS))
        ]
        for j, column in enumerate(columns)
    ]
    wait(first)
    stores = []
    for j, column in enumerate(columns):
        wait(loads[j])
        result = jnp.dot(hidden_t[...], full[:, column], preferred_element_type=jnp.float32)
        product[j] = result.astype(jnp.bfloat16)
        stores.append(copy(product.at[j], product_ref.at[j]))
    wait(stores)


def row_sums(x):
    lanes = 128
    folded = sum(x[:, at] for at in spans(lanes, x.shape[1] // lanes))
    return lax.dot_general(
        jnp.ones((8, lanes), jnp.float32), folded, (((1,), (1,)), ((), ())),
        precision=lax.Precision.HIGHEST, preferred_element_type=jnp.float32,
    )


def early_kernel(
    place_ref, p0, p1, p2, p3, n0, n1, weight_ref, hidden_ref, gate_ref,
    before_ref, grad_ref, partial_ref,
    full, side, next_full, next_side, total, hidden, grad, sems,
):
    copy = Copies(sems)
    rows = total.shape[0] // 2
    width = full.shape[1] // weight_ref.shape[0]
    sides = load_weight(copy, weight_ref, 0, side)
    loads = load_rows(copy, (p0, p1, p2, p3), full)
    sides_next = load_weight(copy, weight_ref, width, next_side)
    for i, made in enumerate(load_rows(copy, (n0, n1), next_full)):
        loads[i] += made + [copy(hidden_ref.at[i], hidden.at[i])]
    stores = []
    wait(sides)
    for i in (2, 3):
        wait(loads[i])
        at, to = slice(i * rows, (i + 1) * rows), slice((i - 2) * rows, (i - 1) * rows)
        total[to, :] = compare_dot(full[at, :], side[...])
        stores.append(copy(total.at[to, :], before_ref.at[to, :]))
    wait(sides_next)
    partial_ref[...] = jnp.zeros(partial_ref.shape, jnp.float32)
    for i in (0, 1):
        wait(loads[i])
        at = slice(i * rows, (i + 1) * rows)
        proj = compare_dot(full[at, :], side[...])
        proj = proj + compare_dot(next_full[at, :], next_side[...])
        owner = jnp.bitwise_xor(place_ref[0], i)
        partial_ref[owner] = row_sums(hidden[i].astype(jnp.float32) * proj)
        grad[i] = (gate_ref[i] * proj).astype(jnp.bfloat16)
        stores.append(copy(grad.at[i], grad_ref.at[owner]))
    wait(stores)


def late_kernel(
    place_ref, p2, p3, weight_ref, before_ref, hidden_ref, gate_ref, early_partial_ref, early_grad,
    grad_ref, partial_ref, full, side, total, hidden, grad, sems,
):
    copy = Copies(sems)
    rows = total.shape[0] // 2
    width = full.shape[1] // weight_ref.shape[0]
    sides = load_weight(copy, weight_ref, width, side)
    loads = load_rows(copy, (p2, p3), full)
    for i, at in enumerate(spans(rows, 2)):
        loads[i].append(copy(before_ref.at[at, :], total.at[at, :]))
        loads[i].append(copy(hidden_ref.at[i + 2], hidden.at[i]))
    partial_ref[...] = early_partial_ref[...]
    wait(sides)
    stores = []
    for i, at in enumerate(spans(rows, 2)):
        wait(loads[i])
        proj = total[at, :] + compare_dot(full[at, :], side[...])
        owner = jnp.bitwise_xor(place_ref[0], i + 2)
        partial_ref[owner] = row_sums(hidden[i].astype(jnp.float32) * proj)
        grad[i] = (gate_ref[i + 2] * proj).astype(jnp.bfloat16)
        stores.append(copy(grad.at[i], grad_ref.at[owner]))
    wait(stores)


def after(x, *others):
    return lax.optimization_barrier((x,) + others)[0]


def local(upstream, router_logits, expert_ids, hidden_saved, down_weight):
    tokens, cols = upstream.shape
    tensor_count = lax.axis_size("tp")
    context_count = lax.axis_size("ctx")
    data_count = lax.axis_size("dp")
    capacity = hidden_saved.shape[0] // context_count
    units = hidden_saved.shape[1]
    rows = EXPERTS * capacity
    total = QUADS * rows
    quad = lax.rem(lax.axis_index("ctx"), QUADS)

    packed, position, gates = pack(expert_ids.T, router_logits.T, upstream, capacity)
    outgoing = packed.reshape(EXPERTS, slab_rows(capacity), cols)
    groups = [[q + QUADS * e for e in range(EXPERTS)] for q in range(QUADS)]
    received = lax.all_to_all(
        outgoing, "ctx", split_axis=0, concat_axis=0, tiled=True, axis_index_groups=groups
    )
    own_rows = received[:, :capacity].reshape(rows, cols)
    gate_line = received[:, capacity, :capacity].reshape(1, rows)

    def swap(x, bit):
        return lax.ppermute(x, "ctx", [(c, c ^ bit) for c in range(context_count)])

    quads = hidden_saved.reshape(EXPERTS, QUADS, capacity, units).transpose(1, 0, 2, 3)
    quads = quads.reshape(QUADS, rows, units)
    hidden = jnp.stack(
        [
            lax.dynamic_index_in_dim(quads, jnp.bitwise_xor(quad, i), 0, keepdims=False)
            for i in range(QUADS)
        ]
    )

    hidden_turned = hidden.reshape(total, units).T
    weight = lax.all_gather(down_weight, "dp", axis=0, tiled=False)
    width = cols // CHUNKS
    sent = [own_rows[:, column] for column in spans(width, CHUNKS)]
    sent[0] = jnp.concatenate([sent[0], jnp.pad(gate_line, ((0, 7), (0, width - rows)))])
    sent[0] = after(sent[0], hidden, hidden_turned)
    gathered = [lax.all_gather(x, "tp", axis=0, tiled=False) for x in sent]
    others = [swap(x, 2) for x in gathered]
    core = [swap(after(x, others[0], *gathered), 1) for x in gathered]
    last_others = swap(after(others[0], *gathered), 1)
    firsts = (gathered[0], core[0], others[0], last_others)

    gate = jnp.stack([piece[0, rows, :rows] for piece in firsts]).astype(jnp.float32)
    hidden_t = (hidden_turned.astype(jnp.float32) * gate.reshape(1, total)).astype(jnp.bfloat16)
    gate_column = gate[:, :, None]

    place = quad.astype(jnp.int32).reshape(1)
    blocks = data_count
    held = pl.BlockSpec(memory_space=pl.ANY)
    vmem = pl.BlockSpec(memory_space=pltpu.VMEM)
    smem = pl.BlockSpec(memory_space=pltpu.SMEM)

    def space(*shape, dtype=jnp.bfloat16):
        return pltpu.VMEM(shape, dtype)

    def call(kernel, outputs, out_specs, scratch, copies, weigh, specs, inputs, aliases={}):
        return pl.pallas_call(
            kernel,
            out_shape=outputs,
            in_specs=specs,
            out_specs=out_specs,
            scratch_shapes=scratch + [pltpu.SemaphoreType.DMA((copies,))],
            input_output_aliases=aliases,
            compiler_params=pltpu.CompilerParams(vmem_limit_bytes=VMEM_LIMIT),
            cost_estimate=pl.CostEstimate(
                flops=weigh, bytes_accessed=1 << 20, transcendentals=0
            ),
        )(*inputs)

    def product_of(pieces, weigh):
        return call(
            product_kernel, jax.ShapeDtypeStruct((blocks, units, width), jnp.bfloat16), held,
            [space(total, blocks * width), space(units, total), space(blocks, units, width)],
            1 + blocks * (QUADS + 1), weigh, [held] * 5, (*pieces, hidden_t),
        )

    def settle(product):
        return lax.psum_scatter(product, "dp", scatter_dimension=0, tiled=False)

    grad_shape = jax.ShapeDtypeStruct((QUADS, rows, units), jnp.bfloat16)
    partial_shape = jax.ShapeDtypeStruct((QUADS, 8, rows), jnp.float32)
    half = total // 2
    half_spaces = [
        space(half, blocks * width), space(units, blocks * width),
        space(half, units, dtype=jnp.float32), space(2, rows, units), space(2, rows, units),
    ]

    product = product_of(firsts, WEIGH[0])
    grads = [settle(product)]
    before, early_grad, early_partial = call(
        early_kernel, (jax.ShapeDtypeStruct((half, units), jnp.float32), grad_shape, partial_shape),
        (held, held, vmem), [space(total, blocks * width), space(units, blocks * width)] + half_spaces,
        blocks * 8 + 6, WEIGH[1], [smem] + [held] * 8 + [vmem],
        (after(place, product), *firsts, gathered[1], core[1], weight, hidden, gate_column),
    )
    lasts = (others[1], swap(after(others[1], before, gate_column), 1))
    product = product_of((gathered[1], core[1], *lasts), WEIGH[2])
    grads.append(settle(product))
    hidden_grad, partial = call(
        late_kernel, (grad_shape, partial_shape), (held, vmem), half_spaces, blocks * 3 + 6,
        1 << 20, [smem] + [held] * 5 + [vmem, vmem, held],
        (after(place, product), *lasts, weight, before, hidden, gate_column, early_partial, early_grad),
        {8: 0},
    )
    down_grad = jnp.concatenate(grads, axis=1)

    def canonical(x):
        x = x.reshape(QUADS, EXPERTS, capacity, -1).transpose(1, 0, 2, 3)
        return x.reshape(context_count * capacity, -1)

    hidden_grad = canonical(hidden_grad)
    sums = partial[:, 0].reshape(QUADS, EXPERTS, capacity).transpose(1, 0, 2)
    sums = sums.reshape(context_count, 1, capacity)
    outgoing_sums = jnp.broadcast_to(sums, (context_count, tensor_count, capacity))
    returned = lax.all_to_all(
        outgoing_sums.reshape(context_count * tensor_count, capacity),
        ("ctx", "tp"), split_axis=0, concat_axis=0, tiled=True,
    )
    expert_sums = returned.reshape(EXPERTS, -1, capacity).sum(axis=1)
    route_grad = jnp.take(expert_sums.reshape(-1), position)
    logit_grad = gates * (route_grad - jnp.sum(gates * route_grad, axis=0, keepdims=True))
    return (hidden_grad, down_grad, logit_grad.T)


def solution(mesh):
    in_specs = (
        P(("dp", "ctx"), "tp"),
        P(("dp", "ctx"), None),
        P(("dp", "ctx"), None),
        P("dp", ("ctx", "tp")),
        P(("ctx", "tp"), "dp"),
    )
    out_specs = (P("dp", ("ctx", "tp")), P(("ctx", "tp"), "dp"), P(("dp", "ctx"), None))
    return jax.shard_map(local, mesh=mesh, in_specs=in_specs, out_specs=out_specs, check_vma=False)
```

```python
import functools

import jax
import jax.numpy as jnp
from jax import lax
from jax.experimental import pallas as pl
from jax.experimental.pallas import tpu as pltpu
from jax.sharding import PartitionSpec as P

EXPERTS = 8
TOP = 2
QUADS = 4
VMEM_LIMIT = 56 * 1024 * 1024
CHUNKS = 2
WEIGH = (1 << 20, 1 << 20, 18 * 10**9)


def compare_dot(a, b):
    return lax.dot_general(a, b, (((1,), (1,)), ((), ())), preferred_element_type=jnp.float32)


def slab_rows(capacity):
    return (capacity // 8 + 1) * 8


def pack_kernel(capacity, ids_ref, logits_ref, upstream_ref, packed_ref, position_ref, gates_ref):
    tokens = upstream_ref.shape[0]
    rows = packed_ref.shape[0]
    per_expert = rows // EXPERTS
    ids = [ids_ref[k : k + 1, :] for k in range(TOP)]
    expert = lax.broadcasted_iota(jnp.int32, (EXPERTS, tokens), 0)
    chosen = [(expert == ids[k]).astype(jnp.float32) for k in range(TOP)]
    before = (
        lax.broadcasted_iota(jnp.int32, (tokens, tokens), 0)
        < lax.broadcasted_iota(jnp.int32, (tokens, tokens), 1)
    ).astype(jnp.bfloat16)
    earlier = jnp.dot(
        (chosen[0] + chosen[1]).astype(jnp.bfloat16), before, preferred_element_type=jnp.float32
    )
    row = lax.broadcasted_iota(jnp.int32, (rows, tokens), 0)
    place = jnp.zeros((rows, tokens), jnp.float32)
    for k in range(TOP):
        slot = jnp.sum(earlier * chosen[k], axis=0, keepdims=True).astype(jnp.int32)
        gate = 1.0 / (1.0 + jnp.exp(logits_ref[1 - k : 2 - k, :] - logits_ref[k : k + 1, :]))
        place = place + jnp.where(row == ids[k] * per_expert + slot, gate, 0.0)
        position_ref[k : k + 1, :] = ids[k] * capacity + slot
        gates_ref[k : k + 1, :] = gate
    packed = jnp.dot(
        place.astype(jnp.bfloat16), upstream_ref[...], preferred_element_type=jnp.float32
    )
    packed_ref[...] = packed.astype(jnp.bfloat16)


def pack(ids, logits, upstream, capacity):
    tokens, cols = upstream.shape
    rows = EXPERTS * slab_rows(capacity)
    return pl.pallas_call(
        functools.partial(pack_kernel, capacity),
        out_shape=(
            jax.ShapeDtypeStruct((rows, cols), jnp.bfloat16),
            jax.ShapeDtypeStruct((TOP, tokens), jnp.int32),
            jax.ShapeDtypeStruct((TOP, tokens), jnp.float32),
        ),
        compiler_params=pltpu.CompilerParams(vmem_limit_bytes=VMEM_LIMIT),
        cost_estimate=pl.CostEstimate(
            flops=2 * rows * tokens * cols, bytes_accessed=2 * (rows + tokens) * cols, transcendentals=0
        ),
    )(ids, logits, upstream)


class Copies:
    def __init__(self, sems):
        self.sems, self.count = sems, 0

    def __call__(self, source, target):
        made = pltpu.make_async_copy(source, target, self.sems.at[self.count])
        self.count += 1
        made.start()
        return made


def spans(size, count):
    return [slice(i * size, (i + 1) * size) for i in range(count)]


def wait(copies):
    for made in copies:
        made.wait()


def load_rows(copy, pieces, full):
    rows, blocks = full.shape[0] // len(pieces), pieces[0].shape[0]
    columns = spans(full.shape[1] // blocks, blocks)
    return [
        [copy(piece.at[j, 0:rows, :], full.at[at, column]) for j, column in enumerate(columns)]
        for piece, at in zip(pieces, spans(rows, len(pieces)))
    ]


def load_weight(copy, weight_ref, start, side):
    blocks = weight_ref.shape[0]
    width = side.shape[1] // blocks
    return [
        copy(weight_ref.at[j, :, start : start + width], side.at[:, column])
        for j, column in enumerate(spans(width, blocks))
    ]


def product_kernel(p0, p1, p2, p3, hidden_t_ref, product_ref, full, hidden_t, product, sems):
    copy = Copies(sems)
    blocks, _, width = product.shape
    rows = full.shape[0] // QUADS
    columns = spans(width, blocks)
    first = [copy(hidden_t_ref, hidden_t)]
    loads = [
        [
            copy(piece.at[j, 0:rows, :], full.at[at, column])
            for piece, at in zip((p0, p1, p2, p3), spans(rows, QUADS))
        ]
        for j, column in enumerate(columns)
    ]
    wait(first)
    stores = []
    for j, column in enumerate(columns):
        wait(loads[j])
        result = jnp.dot(hidden_t[...], full[:, column], preferred_element_type=jnp.float32)
        product[j] = result.astype(jnp.bfloat16)
        stores.append(copy(product.at[j], product_ref.at[j]))
    wait(stores)


def row_sums(x):
    lanes = 128
    folded = sum(x[:, at] for at in spans(lanes, x.shape[1] // lanes))
    return lax.dot_general(
        jnp.ones((8, lanes), jnp.float32), folded, (((1,), (1,)), ((), ())),
        precision=lax.Precision.HIGHEST, preferred_element_type=jnp.float32,
    )


def early_kernel(
    place_ref, p0, p1, p2, p3, n0, n1, weight_ref, hidden_ref,
    before_ref, grad_ref, partial_ref,
    full, side, next_full, next_side, total, hidden, grad, sems,
):
    copy = Copies(sems)
    rows = total.shape[0] // 2
    half = total.shape[0]
    width = full.shape[1] // weight_ref.shape[0]
    sides = load_weight(copy, weight_ref, 0, side)
    loads = load_rows(copy, (p2, p3, p0, p1), full)
    sides_next = load_weight(copy, weight_ref, width, next_side)
    for i, made in enumerate(load_rows(copy, (n0, n1), next_full)):
        loads[i + 2] += made + [copy(hidden_ref.at[i], hidden.at[i])]
    stores = []
    wait(sides)
    for i, at in enumerate(spans(rows, 2)):
        wait(loads[i])
        total[at, :] = compare_dot(full[at, :], side[...])
        stores.append(copy(total.at[at, :], before_ref.at[at, :]))
    wait(sides_next)
    partial_ref[...] = jnp.zeros(partial_ref.shape, jnp.float32)
    for i, at in enumerate(spans(rows, 2)):
        wait(loads[i + 2])
        proj = compare_dot(full[half + i * rows : half + (i + 1) * rows, :], side[...])
        proj = proj + compare_dot(next_full[at, :], next_side[...])
        owner = jnp.bitwise_xor(place_ref[0], i)
        partial_ref[owner] = row_sums(hidden[i].astype(jnp.float32) * proj)
        grad[i] = proj.astype(jnp.bfloat16)
        stores.append(copy(grad.at[i], grad_ref.at[owner]))
    wait(stores)


def late_kernel(
    place_ref, p2, p3, weight_ref, before_ref, hidden_ref, early_partial_ref, early_grad,
    grad_ref, partial_ref, full, side, total, hidden, grad, sems,
):
    copy = Copies(sems)
    rows = total.shape[0] // 2
    width = full.shape[1] // weight_ref.shape[0]
    sides = load_weight(copy, weight_ref, width, side)
    loads = load_rows(copy, (p2, p3), full)
    for i, at in enumerate(spans(rows, 2)):
        loads[i].append(copy(before_ref.at[at, :], total.at[at, :]))
        loads[i].append(copy(hidden_ref.at[i + 2], hidden.at[i]))
    partial_ref[...] = early_partial_ref[...]
    wait(sides)
    stores = []
    for i, at in enumerate(spans(rows, 2)):
        wait(loads[i])
        proj = total[at, :] + compare_dot(full[at, :], side[...])
        owner = jnp.bitwise_xor(place_ref[0], i + 2)
        partial_ref[owner] = row_sums(hidden[i].astype(jnp.float32) * proj)
        grad[i] = proj.astype(jnp.bfloat16)
        stores.append(copy(grad.at[i], grad_ref.at[owner]))
    wait(stores)


def join_kernel(a_ref, b_ref, out_ref, sems):
    copy = Copies(sems)
    columns = spans(a_ref.shape[1], CHUNKS)
    wait([copy(ref, out_ref.at[:, column]) for ref, column in zip((a_ref, b_ref), columns)])


def after(x, *others):
    return lax.optimization_barrier((x,) + others)[0]


def local(upstream, router_logits, expert_ids, hidden_saved, down_weight):
    tokens, cols = upstream.shape
    tensor_count = lax.axis_size("tp")
    context_count = lax.axis_size("ctx")
    data_count = lax.axis_size("dp")
    capacity = hidden_saved.shape[0] // context_count
    units = hidden_saved.shape[1]
    rows = EXPERTS * capacity
    total = QUADS * rows
    quad = lax.rem(lax.axis_index("ctx"), QUADS)

    packed, position, gates = pack(expert_ids.T, router_logits.T, upstream, capacity)
    outgoing = packed.reshape(EXPERTS, slab_rows(capacity), cols)
    groups = [[q + QUADS * e for e in range(EXPERTS)] for q in range(QUADS)]
    received = lax.all_to_all(
        outgoing, "ctx", split_axis=0, concat_axis=0, tiled=True, axis_index_groups=groups
    )
    own_rows = received[:, :capacity].reshape(rows, cols)

    def swap(x, bit):
        return lax.ppermute(x, "ctx", [(c, c ^ bit) for c in range(context_count)])

    quads = hidden_saved.reshape(EXPERTS, QUADS, capacity, units).transpose(1, 0, 2, 3)
    quads = quads.reshape(QUADS, rows, units)
    hidden = jnp.stack(
        [
            lax.dynamic_index_in_dim(quads, jnp.bitwise_xor(quad, i), 0, keepdims=False)
            for i in range(QUADS)
        ]
    )

    hidden_t = hidden.reshape(total, units).T
    weight = lax.all_gather(down_weight, "dp", axis=0, tiled=False)
    width = cols // CHUNKS
    sent = [own_rows[:, column] for column in spans(width, CHUNKS)]
    sent[0] = after(sent[0], hidden, hidden_t)
    gathered = [lax.all_gather(x, "tp", axis=0, tiled=False) for x in sent]
    others = [swap(x, 2) for x in gathered]
    core = [swap(after(x, others[0], *gathered), 1) for x in gathered]
    last_others = swap(after(others[0], *gathered), 1)
    firsts = (gathered[0], core[0], others[0], last_others)

    place = quad.astype(jnp.int32).reshape(1)
    blocks = data_count
    held = pl.BlockSpec(memory_space=pl.ANY)
    vmem = pl.BlockSpec(memory_space=pltpu.VMEM)
    smem = pl.BlockSpec(memory_space=pltpu.SMEM)

    def space(*shape, dtype=jnp.bfloat16):
        return pltpu.VMEM(shape, dtype)

    def call(kernel, outputs, out_specs, scratch, copies, weigh, specs, inputs, aliases={}):
        return pl.pallas_call(
            kernel,
            out_shape=outputs,
            in_specs=specs,
            out_specs=out_specs,
            scratch_shapes=scratch + [pltpu.SemaphoreType.DMA((copies,))],
            input_output_aliases=aliases,
            compiler_params=pltpu.CompilerParams(vmem_limit_bytes=VMEM_LIMIT),
            cost_estimate=pl.CostEstimate(
                flops=weigh, bytes_accessed=1 << 20, transcendentals=0
            ),
        )(*inputs)

    def product_of(pieces, weigh):
        return call(
            product_kernel, jax.ShapeDtypeStruct((blocks, units, width), jnp.bfloat16), held,
            [space(total, blocks * width), space(units, total), space(blocks, units, width)],
            1 + blocks * (QUADS + 1), weigh, [held] * 5, (*pieces, hidden_t),
        )

    def settle(product):
        return lax.psum_scatter(product, "dp", scatter_dimension=0, tiled=False)

    grad_shape = jax.ShapeDtypeStruct((QUADS, rows, units), jnp.bfloat16)
    partial_shape = jax.ShapeDtypeStruct((QUADS, 8, rows), jnp.float32)
    half = total // 2
    half_spaces = [
        space(half, blocks * width), space(units, blocks * width),
        space(half, units, dtype=jnp.float32), space(2, rows, units), space(2, rows, units),
    ]

    product = product_of(firsts, WEIGH[0])
    grads = [settle(product)]
    before, early_grad, early_partial = call(
        early_kernel, (jax.ShapeDtypeStruct((half, units), jnp.float32), grad_shape, partial_shape),
        (held, held, vmem), [space(total, blocks * width), space(units, blocks * width)] + half_spaces,
        blocks * 8 + 6, WEIGH[1], [smem] + [held] * 8,
        (after(place, product), *firsts, gathered[1], core[1], weight, hidden),
    )
    lasts = (others[1], swap(after(others[1], before), 1))
    product = product_of((gathered[1], core[1], *lasts), WEIGH[2])
    grads.append(settle(product))
    hidden_grad, partial = call(
        late_kernel, (grad_shape, partial_shape), (held, vmem), half_spaces, blocks * 3 + 6,
        1 << 20, [smem] + [held] * 5 + [vmem, held],
        (after(place, product), *lasts, weight, before, hidden, early_partial, early_grad),
        {7: 0},
    )
    down_grad = call(
        join_kernel, jax.ShapeDtypeStruct((units, cols), jnp.bfloat16), held, [], CHUNKS, 1 << 20,
        [held] * CHUNKS, grads,
    )

    def canonical(x):
        x = x.reshape(QUADS, EXPERTS, capacity, -1).transpose(1, 0, 2, 3)
        return x.reshape(context_count * capacity, -1)

    hidden_grad = canonical(hidden_grad)
    sums = partial[:, 0].reshape(QUADS, EXPERTS, capacity).transpose(1, 0, 2)
    sums = sums.reshape(context_count, 1, capacity)
    outgoing_sums = jnp.broadcast_to(sums, (context_count, tensor_count, capacity))
    returned = lax.all_to_all(
        outgoing_sums.reshape(context_count * tensor_count, capacity),
        ("ctx", "tp"), split_axis=0, concat_axis=0, tiled=True,
    )
    expert_sums = returned.reshape(EXPERTS, -1, capacity).sum(axis=1)
    gates_sent = gates.astype(jnp.bfloat16).astype(jnp.float32)
    route_grad = jnp.take(expert_sums.reshape(-1), position) / gates_sent
    logit_grad = gates * (route_grad - jnp.sum(gates * route_grad, axis=0, keepdims=True))
    return (hidden_grad, down_grad, logit_grad.T)


def solution(mesh):
    in_specs = (
        P(("dp", "ctx"), "tp"),
        P(("dp", "ctx"), None),
        P(("dp", "ctx"), None),
        P("dp", ("ctx", "tp")),
        P(("ctx", "tp"), "dp"),
    )
    out_specs = (P("dp", ("ctx", "tp")), P(("ctx", "tp"), "dp"), P(("dp", "ctx"), None))
    return jax.shard_map(local, mesh=mesh, in_specs=in_specs, out_specs=out_specs, check_vma=False)
```

```python
import functools

import jax
import jax.numpy as jnp
from jax import lax
from jax.experimental import pallas as pl
from jax.experimental.pallas import tpu as pltpu
from jax.sharding import PartitionSpec as P

EXPERTS = 8
TOP = 2
QUADS = 4
VMEM_LIMIT = 56 * 1024 * 1024
CHUNKS = 2
WEIGH = (1 << 20, 1 << 20, 18 * 10**9)


def compare_dot(a, b):
    return lax.dot_general(a, b, (((1,), (1,)), ((), ())), preferred_element_type=jnp.float32)


def slab_rows(capacity):
    return (capacity // 8 + 1) * 8


def pack_kernel(capacity, ids_ref, logits_ref, upstream_ref, packed_ref, position_ref, gates_ref):
    tokens = upstream_ref.shape[0]
    rows = packed_ref.shape[0]
    per_expert = rows // EXPERTS
    ids = [ids_ref[k : k + 1, :] for k in range(TOP)]
    expert = lax.broadcasted_iota(jnp.int32, (EXPERTS, tokens), 0)
    chosen = [(expert == ids[k]).astype(jnp.float32) for k in range(TOP)]
    before = (
        lax.broadcasted_iota(jnp.int32, (tokens, tokens), 0)
        < lax.broadcasted_iota(jnp.int32, (tokens, tokens), 1)
    ).astype(jnp.bfloat16)
    earlier = jnp.dot(
        (chosen[0] + chosen[1]).astype(jnp.bfloat16), before, preferred_element_type=jnp.float32
    )
    row = lax.broadcasted_iota(jnp.int32, (rows, tokens), 0)
    place = jnp.zeros((rows, tokens), jnp.float32)
    for k in range(TOP):
        slot = jnp.sum(earlier * chosen[k], axis=0, keepdims=True).astype(jnp.int32)
        gate = 1.0 / (1.0 + jnp.exp(logits_ref[1 - k : 2 - k, :] - logits_ref[k : k + 1, :]))
        place = place + jnp.where(row == ids[k] * per_expert + slot, gate, 0.0)
        position_ref[k : k + 1, :] = ids[k] * capacity + slot
        gates_ref[k : k + 1, :] = gate
    packed = jnp.dot(
        place.astype(jnp.bfloat16), upstream_ref[...], preferred_element_type=jnp.float32
    )
    packed_ref[...] = packed.astype(jnp.bfloat16)


def pack(ids, logits, upstream, capacity):
    tokens, cols = upstream.shape
    rows = EXPERTS * slab_rows(capacity)
    return pl.pallas_call(
        functools.partial(pack_kernel, capacity),
        out_shape=(
            jax.ShapeDtypeStruct((rows, cols), jnp.bfloat16),
            jax.ShapeDtypeStruct((TOP, tokens), jnp.int32),
            jax.ShapeDtypeStruct((TOP, tokens), jnp.float32),
        ),
        compiler_params=pltpu.CompilerParams(vmem_limit_bytes=VMEM_LIMIT),
        cost_estimate=pl.CostEstimate(
            flops=2 * rows * tokens * cols, bytes_accessed=2 * (rows + tokens) * cols, transcendentals=0
        ),
    )(ids, logits, upstream)


class Copies:
    def __init__(self, sems):
        self.sems, self.count = sems, 0

    def __call__(self, source, target):
        made = pltpu.make_async_copy(source, target, self.sems.at[self.count])
        self.count += 1
        made.start()
        return made


def spans(size, count):
    return [slice(i * size, (i + 1) * size) for i in range(count)]


def wait(copies):
    for made in copies:
        made.wait()


def load_rows(copy, pieces, full):
    rows, blocks = full.shape[0] // len(pieces), pieces[0].shape[0]
    columns = spans(full.shape[1] // blocks, blocks)
    return [
        [copy(piece.at[j, 0:rows, :], full.at[at, column]) for j, column in enumerate(columns)]
        for piece, at in zip(pieces, spans(rows, len(pieces)))
    ]


def load_weight(copy, weight_ref, start, side):
    blocks = weight_ref.shape[0]
    width = side.shape[1] // blocks
    return [
        copy(weight_ref.at[j, :, start : start + width], side.at[:, column])
        for j, column in enumerate(spans(width, blocks))
    ]


def product_kernel(p0, p1, p2, p3, hidden_t_ref, product_ref, full, hidden_t, product, sems):
    copy = Copies(sems)
    blocks, _, width = product.shape
    rows = full.shape[0] // QUADS
    columns = spans(width, blocks)
    first = [copy(hidden_t_ref, hidden_t)]
    loads = [
        [
            copy(piece.at[j, 0:rows, :], full.at[at, column])
            for piece, at in zip((p0, p1, p2, p3), spans(rows, QUADS))
        ]
        for j, column in enumerate(columns)
    ]
    wait(first)
    stores = []
    for j, column in enumerate(columns):
        wait(loads[j])
        result = jnp.dot(hidden_t[...], full[:, column], preferred_element_type=jnp.float32)
        product[j] = result.astype(jnp.bfloat16)
        stores.append(copy(product.at[j], product_ref.at[j]))
    wait(stores)


def row_sums(x):
    lanes = 128
    folded = sum(x[:, at] for at in spans(lanes, x.shape[1] // lanes))
    return lax.dot_general(
        jnp.ones((8, lanes), jnp.float32), folded, (((1,), (1,)), ((), ())),
        precision=lax.Precision.HIGHEST, preferred_element_type=jnp.float32,
    )


def early_kernel(
    place_ref, p0, p1, p2, p3, n0, weight_ref, hidden_ref,
    before_ref, grad_ref, partial_ref,
    full, side, next_full, next_side, total, hidden, grad, sems,
):
    copy = Copies(sems)
    rows = next_full.shape[0]
    width = full.shape[1] // weight_ref.shape[0]
    sides = load_weight(copy, weight_ref, 0, side)
    loads = load_rows(copy, (p0, p1, p2, p3), full)
    sides_next = load_weight(copy, weight_ref, width, next_side)
    loads_next = load_rows(copy, (n0,), next_full)[0] + [copy(hidden_ref.at[0], hidden)]
    stores = []
    wait(sides)
    for i, at in enumerate(spans(rows, QUADS)):
        wait(loads[i])
        total[at, :] = compare_dot(full[at, :], side[...])
        if i:
            to = slice((i - 1) * rows, i * rows)
            stores.append(copy(total.at[at, :], before_ref.at[to, :]))
    wait(sides_next + loads_next)
    proj = total[:rows, :] + compare_dot(next_full[...], next_side[...])
    owner = place_ref[0]
    partial_ref[...] = jnp.zeros(partial_ref.shape, jnp.float32)
    partial_ref[owner] = row_sums(hidden[...].astype(jnp.float32) * proj)
    grad[...] = proj.astype(jnp.bfloat16)
    stores.append(copy(grad, grad_ref.at[owner]))
    wait(stores)


def late_kernel(
    place_ref, p1, p2, p3, weight_ref, before_ref, hidden_ref, early_partial_ref, early_grad,
    grad_ref, partial_ref, full, side, total, hidden, grad, sems,
):
    copy = Copies(sems)
    late = QUADS - 1
    rows = full.shape[0] // late
    width = full.shape[1] // weight_ref.shape[0]
    sides = load_weight(copy, weight_ref, width, side)
    loads = load_rows(copy, (p1, p2, p3), full)
    for i, at in enumerate(spans(rows, late)):
        loads[i].append(copy(before_ref.at[at, :], total.at[at, :]))
        loads[i].append(copy(hidden_ref.at[i + 1], hidden.at[i]))
    partial_ref[...] = early_partial_ref[...]
    wait(sides)
    stores = []
    for i, at in enumerate(spans(rows, late)):
        wait(loads[i])
        proj = total[at, :] + compare_dot(full[at, :], side[...])
        owner = jnp.bitwise_xor(place_ref[0], i + 1)
        partial_ref[owner] = row_sums(hidden[i].astype(jnp.float32) * proj)
        grad[i] = proj.astype(jnp.bfloat16)
        stores.append(copy(grad.at[i], grad_ref.at[owner]))
    wait(stores)


def join_kernel(a_ref, b_ref, out_ref):
    width = a_ref.shape[1]
    out_ref[:, :width] = a_ref[...]
    out_ref[:, width:] = b_ref[...]


def after(x, *others):
    return lax.optimization_barrier((x,) + others)[0]


def local(upstream, router_logits, expert_ids, hidden_saved, down_weight):
    tokens, cols = upstream.shape
    tensor_count = lax.axis_size("tp")
    context_count = lax.axis_size("ctx")
    data_count = lax.axis_size("dp")
    capacity = hidden_saved.shape[0] // context_count
    units = hidden_saved.shape[1]
    rows = EXPERTS * capacity
    total = QUADS * rows
    quad = lax.rem(lax.axis_index("ctx"), QUADS)

    packed, position, gates = pack(expert_ids.T, router_logits.T, upstream, capacity)
    outgoing = packed.reshape(EXPERTS, slab_rows(capacity), cols)
    groups = [[q + QUADS * e for e in range(EXPERTS)] for q in range(QUADS)]
    received = lax.all_to_all(
        outgoing, "ctx", split_axis=0, concat_axis=0, tiled=True, axis_index_groups=groups
    )
    own_rows = received[:, :capacity].reshape(rows, cols)

    def swap(x, bit):
        return lax.ppermute(x, "ctx", [(c, c ^ bit) for c in range(context_count)])

    quads = hidden_saved.reshape(EXPERTS, QUADS, capacity, units).transpose(1, 0, 2, 3)
    quads = quads.reshape(QUADS, rows, units)
    hidden = jnp.stack(
        [
            lax.dynamic_index_in_dim(quads, jnp.bitwise_xor(quad, i), 0, keepdims=False)
            for i in range(QUADS)
        ]
    )

    hidden_t = hidden.reshape(total, units).T
    weight = lax.all_gather(down_weight, "dp", axis=0, tiled=False)
    width = cols // CHUNKS
    sent = [own_rows[:, column] for column in spans(width, CHUNKS)]
    sent[0] = after(sent[0], hidden, hidden_t)
    gathered = [lax.all_gather(x, "tp", axis=0, tiled=False) for x in sent]
    others = [swap(x, 2) for x in gathered]
    core = [swap(after(x, others[0], *gathered), 1) for x in gathered]
    last_others = swap(after(others[0], *gathered), 1)
    firsts = (gathered[0], core[0], others[0], last_others)

    place = quad.astype(jnp.int32).reshape(1)
    blocks = data_count
    held = pl.BlockSpec(memory_space=pltpu.HBM)
    vmem = pl.BlockSpec(memory_space=pltpu.VMEM)
    smem = pl.BlockSpec(memory_space=pltpu.SMEM)

    def space(*shape, dtype=jnp.bfloat16):
        return pltpu.VMEM(shape, dtype)

    def call(kernel, outputs, out_specs, scratch, copies, weigh, specs, inputs, aliases={}):
        return pl.pallas_call(
            kernel,
            out_shape=outputs,
            in_specs=specs,
            out_specs=out_specs,
            scratch_shapes=scratch + [pltpu.SemaphoreType.DMA((copies,))],
            input_output_aliases=aliases,
            compiler_params=pltpu.CompilerParams(vmem_limit_bytes=VMEM_LIMIT),
            cost_estimate=pl.CostEstimate(
                flops=weigh, bytes_accessed=1 << 20, transcendentals=0
            ),
        )(*inputs)

    def product_of(pieces, weigh):
        return call(
            product_kernel, jax.ShapeDtypeStruct((blocks, units, width), jnp.bfloat16), held,
            [space(total, blocks * width), space(units, total), space(blocks, units, width)],
            1 + blocks * (QUADS + 1), weigh, [held] * 5, (*pieces, hidden_t),
        )

    def settle(product):
        return lax.psum_scatter(product, "dp", scatter_dimension=0, tiled=False)

    grad_shape = jax.ShapeDtypeStruct((QUADS, rows, units), jnp.bfloat16)
    partial_shape = jax.ShapeDtypeStruct((QUADS, 8, rows), jnp.float32)
    late = total - rows
    product = product_of(firsts, WEIGH[0])
    grads = [settle(product)]
    before, early_grad, early_partial = call(
        early_kernel, (jax.ShapeDtypeStruct((late, units), jnp.float32), grad_shape, partial_shape),
        (held, held, vmem),
        [
            space(total, blocks * width), space(units, blocks * width),
            space(rows, blocks * width), space(units, blocks * width),
            space(total, units, dtype=jnp.float32), space(rows, units), space(rows, units),
        ],
        blocks * (QUADS + 3) + 1 + QUADS, WEIGH[1], [smem] + [held] * 7,
        (after(place, product), *firsts, gathered[1], weight, hidden),
    )
    lasts = (core[1], others[1], swap(after(others[1], before), 1))
    product = product_of((gathered[1], *lasts), WEIGH[2])
    grads.append(settle(product))
    hidden_grad, partial = call(
        late_kernel, (grad_shape, partial_shape), (held, vmem),
        [
            space(late, blocks * width), space(units, blocks * width),
            space(late, units, dtype=jnp.float32),
            space(QUADS - 1, rows, units), space(QUADS - 1, rows, units),
        ],
        blocks * QUADS + 3 * (QUADS - 1), 1 << 20, [smem] + [held] * 6 + [vmem, held],
        (after(place, product), *lasts, weight, before, hidden, early_partial, early_grad),
        {8: 0},
    )
    down_grad = pl.pallas_call(
        join_kernel,
        out_shape=jax.ShapeDtypeStruct((units, cols), jnp.bfloat16),
        compiler_params=pltpu.CompilerParams(vmem_limit_bytes=VMEM_LIMIT),
    )(*grads)

    def canonical(x):
        x = x.reshape(QUADS, EXPERTS, capacity, -1).transpose(1, 0, 2, 3)
        return x.reshape(context_count * capacity, -1)

    hidden_grad = canonical(hidden_grad)
    sums = partial[:, 0].reshape(QUADS, EXPERTS, capacity).transpose(1, 0, 2)
    sums = sums.reshape(context_count, 1, capacity)
    outgoing_sums = jnp.broadcast_to(sums, (context_count, tensor_count, capacity))
    returned = lax.all_to_all(
        outgoing_sums.reshape(context_count * tensor_count, capacity),
        ("ctx", "tp"), split_axis=0, concat_axis=0, tiled=True,
    )
    expert_sums = returned.reshape(EXPERTS, -1, capacity).sum(axis=1)
    gates_sent = gates.astype(jnp.bfloat16).astype(jnp.float32)
    route_grad = jnp.take(expert_sums.reshape(-1), position) / gates_sent
    logit_grad = gates * (route_grad - jnp.sum(gates * route_grad, axis=0, keepdims=True))
    return (hidden_grad, down_grad, logit_grad.T)


def solution(mesh):
    in_specs = (
        P(("dp", "ctx"), "tp"),
        P(("dp", "ctx"), None),
        P(("dp", "ctx"), None),
        P("dp", ("ctx", "tp")),
        P(("ctx", "tp"), "dp"),
    )
    out_specs = (P("dp", ("ctx", "tp")), P(("ctx", "tp"), "dp"), P(("dp", "ctx"), None))
    return jax.shard_map(local, mesh=mesh, in_specs=in_specs, out_specs=out_specs, check_vma=False)
```

```python
import functools

import jax
import jax.numpy as jnp
from jax import lax
from jax.experimental import pallas as pl
from jax.experimental.pallas import tpu as pltpu
from jax.sharding import PartitionSpec as P

EXPERTS = 8
TOP = 2
QUADS = 4
VMEM_LIMIT = 48 * 1024 * 1024
CHUNKS = 2
WEIGH = (1 << 20, 1 << 20, 18 * 10**9)


def compare_dot(a, b):
    return lax.dot_general(a, b, (((1,), (1,)), ((), ())), preferred_element_type=jnp.float32)


def slab_rows(capacity):
    return (capacity // 8 + 1) * 8


def pack_kernel(capacity, ids_ref, logits_ref, upstream_ref, packed_ref, position_ref, gates_ref):
    tokens = upstream_ref.shape[0]
    rows = packed_ref.shape[0]
    per_expert = rows // EXPERTS
    ids = [ids_ref[k : k + 1, :] for k in range(TOP)]
    expert = lax.broadcasted_iota(jnp.int32, (EXPERTS, tokens), 0)
    chosen = [(expert == ids[k]).astype(jnp.float32) for k in range(TOP)]
    before = (
        lax.broadcasted_iota(jnp.int32, (tokens, tokens), 0)
        < lax.broadcasted_iota(jnp.int32, (tokens, tokens), 1)
    ).astype(jnp.bfloat16)
    earlier = jnp.dot(
        (chosen[0] + chosen[1]).astype(jnp.bfloat16), before, preferred_element_type=jnp.float32
    )
    row = lax.broadcasted_iota(jnp.int32, (rows, tokens), 0)
    place = jnp.zeros((rows, tokens), jnp.float32)
    for k in range(TOP):
        slot = jnp.sum(earlier * chosen[k], axis=0, keepdims=True).astype(jnp.int32)
        gate = 1.0 / (1.0 + jnp.exp(logits_ref[1 - k : 2 - k, :] - logits_ref[k : k + 1, :]))
        place = place + jnp.where(row == ids[k] * per_expert + slot, gate, 0.0)
        position_ref[k : k + 1, :] = ids[k] * capacity + slot
        gates_ref[k : k + 1, :] = gate
    packed = jnp.dot(
        place.astype(jnp.bfloat16), upstream_ref[...], preferred_element_type=jnp.float32
    )
    packed_ref[...] = packed.astype(jnp.bfloat16)


def pack(ids, logits, upstream, capacity):
    tokens, cols = upstream.shape
    rows = EXPERTS * slab_rows(capacity)
    return pl.pallas_call(
        functools.partial(pack_kernel, capacity),
        out_shape=(
            jax.ShapeDtypeStruct((rows, cols), jnp.bfloat16),
            jax.ShapeDtypeStruct((TOP, tokens), jnp.int32),
            jax.ShapeDtypeStruct((TOP, tokens), jnp.float32),
        ),
        compiler_params=pltpu.CompilerParams(vmem_limit_bytes=VMEM_LIMIT),
        cost_estimate=pl.CostEstimate(
            flops=2 * rows * tokens * cols, bytes_accessed=2 * (rows + tokens) * cols, transcendentals=0
        ),
    )(ids, logits, upstream)


class Copies:
    def __init__(self, sems):
        self.sems, self.count = sems, 0

    def __call__(self, source, target):
        made = pltpu.make_async_copy(source, target, self.sems.at[self.count])
        self.count += 1
        made.start()
        return made


def spans(size, count):
    return [slice(i * size, (i + 1) * size) for i in range(count)]


def wait(copies):
    for made in copies:
        made.wait()


def load_rows(copy, pieces, full):
    rows, blocks = full.shape[0] // len(pieces), pieces[0].shape[0]
    columns = spans(full.shape[1] // blocks, blocks)
    return [
        [copy(piece.at[j, 0:rows, :], full.at[at, column]) for j, column in enumerate(columns)]
        for piece, at in zip(pieces, spans(rows, len(pieces)))
    ]


def load_weight(copy, weight_ref, start, side):
    blocks = weight_ref.shape[0]
    width = side.shape[1] // blocks
    return [
        copy(weight_ref.at[j, :, start : start + width], side.at[:, column])
        for j, column in enumerate(spans(width, blocks))
    ]


def product_kernel(p0, p1, p2, p3, hidden_t_ref, product_ref, full, hidden_t, product, sems):
    copy = Copies(sems)
    blocks, _, width = product.shape
    rows = full.shape[0] // QUADS
    columns = spans(width, blocks)
    first = [copy(hidden_t_ref, hidden_t)]
    loads = [
        [
            copy(piece.at[j, 0:rows, :], full.at[at, column])
            for piece, at in zip((p0, p1, p2, p3), spans(rows, QUADS))
        ]
        for j, column in enumerate(columns)
    ]
    wait(first)
    stores = []
    for j, column in enumerate(columns):
        wait(loads[j])
        result = jnp.dot(hidden_t[...], full[:, column], preferred_element_type=jnp.float32)
        product[j] = result.astype(jnp.bfloat16)
        stores.append(copy(product.at[j], product_ref.at[j]))
    wait(stores)


def row_sums(x):
    lanes = 128
    folded = sum(x[:, at] for at in spans(lanes, x.shape[1] // lanes))
    return lax.dot_general(
        jnp.ones((8, lanes), jnp.float32), folded, (((1,), (1,)), ((), ())),
        precision=lax.Precision.HIGHEST, preferred_element_type=jnp.float32,
    )


def early_kernel(
    place_ref, p0, p1, p2, p3, n0, weight_ref, hidden_ref,
    before_ref, grad_ref, partial_ref,
    full, side, next_full, next_side, total, hidden, grad, sems,
):
    copy = Copies(sems)
    rows = next_full.shape[0]
    width = full.shape[1] // weight_ref.shape[0]
    sides = load_weight(copy, weight_ref, 0, side)
    loads = load_rows(copy, (p0, p1, p2, p3), full)
    sides_next = load_weight(copy, weight_ref, width, next_side)
    loads_next = load_rows(copy, (n0,), next_full)[0] + [copy(hidden_ref.at[0], hidden)]
    stores = []
    wait(sides)
    for i, at in enumerate(spans(rows, QUADS)):
        wait(loads[i])
        total[at, :] = compare_dot(full[at, :], side[...])
        if i:
            to = slice((i - 1) * rows, i * rows)
            stores.append(copy(total.at[at, :], before_ref.at[to, :]))
    wait(sides_next + loads_next)
    proj = total[:rows, :] + compare_dot(next_full[...], next_side[...])
    owner = place_ref[0]
    partial_ref[...] = jnp.zeros(partial_ref.shape, jnp.float32)
    partial_ref[owner] = row_sums(hidden[...].astype(jnp.float32) * proj)
    grad[...] = proj.astype(jnp.bfloat16)
    stores.append(copy(grad, grad_ref.at[owner]))
    wait(stores)


def late_kernel(
    place_ref, p1, p2, p3, weight_ref, before_ref, hidden_ref, early_partial_ref, early_grad,
    grad_ref, partial_ref, full, side, total, hidden, grad, sems,
):
    copy = Copies(sems)
    late = QUADS - 1
    rows = full.shape[0] // late
    width = full.shape[1] // weight_ref.shape[0]
    sides = load_weight(copy, weight_ref, width, side)
    loads = load_rows(copy, (p1, p2, p3), full)
    for i, at in enumerate(spans(rows, late)):
        loads[i].append(copy(before_ref.at[at, :], total.at[at, :]))
        loads[i].append(copy(hidden_ref.at[i + 1], hidden.at[i]))
    partial_ref[...] = early_partial_ref[...]
    wait(sides)
    stores = []
    for i, at in enumerate(spans(rows, late)):
        wait(loads[i])
        proj = total[at, :] + compare_dot(full[at, :], side[...])
        owner = jnp.bitwise_xor(place_ref[0], i + 1)
        partial_ref[owner] = row_sums(hidden[i].astype(jnp.float32) * proj)
        grad[i] = proj.astype(jnp.bfloat16)
        stores.append(copy(grad.at[i], grad_ref.at[owner]))
    wait(stores)


def join_kernel(a_ref, b_ref, out_ref, whole, sems):
    copy = Copies(sems)
    columns, parts = spans(a_ref.shape[1], CHUNKS), spans(a_ref.shape[0] // 2, 2)
    loads = [
        [copy(ref.at[at, :], whole.at[at, c]) for ref, c in zip((a_ref, b_ref), columns)]
        for at in parts
    ]
    stores = []
    for made, at in zip(loads, parts):
        wait(made)
        stores.append(copy(whole.at[at, :], out_ref.at[at, :]))
    wait(stores)


def after(x, *others):
    return lax.optimization_barrier((x,) + others)[0]


def local(upstream, router_logits, expert_ids, hidden_saved, down_weight):
    tokens, cols = upstream.shape
    tensor_count = lax.axis_size("tp")
    context_count = lax.axis_size("ctx")
    data_count = lax.axis_size("dp")
    capacity = hidden_saved.shape[0] // context_count
    units = hidden_saved.shape[1]
    rows = EXPERTS * capacity
    total = QUADS * rows
    quad = lax.rem(lax.axis_index("ctx"), QUADS)

    packed, position, gates = pack(expert_ids.T, router_logits.T, upstream, capacity)
    outgoing = packed.reshape(EXPERTS, slab_rows(capacity), cols)
    groups = [[q + QUADS * e for e in range(EXPERTS)] for q in range(QUADS)]
    received = lax.all_to_all(
        outgoing, "ctx", split_axis=0, concat_axis=0, tiled=True, axis_index_groups=groups
    )
    own_rows = received[:, :capacity].reshape(rows, cols)

    def swap(x, bit):
        return lax.ppermute(x, "ctx", [(c, c ^ bit) for c in range(context_count)])

    quads = hidden_saved.reshape(EXPERTS, QUADS, capacity, units).transpose(1, 0, 2, 3)
    quads = quads.reshape(QUADS, rows, units)
    hidden = jnp.stack(
        [
            lax.dynamic_index_in_dim(quads, jnp.bitwise_xor(quad, i), 0, keepdims=False)
            for i in range(QUADS)
        ]
    )

    hidden_t = hidden.reshape(total, units).T
    weight = lax.all_gather(down_weight, "dp", axis=0, tiled=False)
    width = cols // CHUNKS
    sent = [own_rows[:, column] for column in spans(width, CHUNKS)]
    sent[0] = after(sent[0], hidden, hidden_t)
    gathered = [lax.all_gather(x, "tp", axis=0, tiled=False) for x in sent]
    others = [swap(x, 2) for x in gathered]
    core = [swap(after(x, others[0], *gathered), 1) for x in gathered]
    last_others = swap(after(others[0], *gathered), 1)
    firsts = (gathered[0], core[0], others[0], last_others)

    place = quad.astype(jnp.int32).reshape(1)
    blocks = data_count
    held = pl.BlockSpec(memory_space=pltpu.HBM)
    vmem = pl.BlockSpec(memory_space=pltpu.VMEM)
    smem = pl.BlockSpec(memory_space=pltpu.SMEM)

    def space(*shape, dtype=jnp.bfloat16):
        return pltpu.VMEM(shape, dtype)

    def call(kernel, outputs, out_specs, scratch, copies, weigh, specs, inputs, aliases={}):
        return pl.pallas_call(
            kernel,
            out_shape=outputs,
            in_specs=specs,
            out_specs=out_specs,
            scratch_shapes=scratch + [pltpu.SemaphoreType.DMA((copies,))],
            input_output_aliases=aliases,
            compiler_params=pltpu.CompilerParams(vmem_limit_bytes=VMEM_LIMIT),
            cost_estimate=pl.CostEstimate(
                flops=weigh, bytes_accessed=1 << 20, transcendentals=0
            ),
        )(*inputs)

    def product_of(pieces, weigh):
        return call(
            product_kernel, jax.ShapeDtypeStruct((blocks, units, width), jnp.bfloat16), held,
            [space(total, blocks * width), space(units, total), space(blocks, units, width)],
            1 + blocks * (QUADS + 1), weigh, [held] * 5, (*pieces, hidden_t),
        )

    def settle(product):
        return lax.psum_scatter(product, "dp", scatter_dimension=0, tiled=False)

    grad_shape = jax.ShapeDtypeStruct((QUADS, rows, units), jnp.bfloat16)
    partial_shape = jax.ShapeDtypeStruct((QUADS, 8, rows), jnp.float32)
    late = total - rows
    product = product_of(firsts, WEIGH[0])
    grads = [settle(product)]
    before, early_grad, early_partial = call(
        early_kernel, (jax.ShapeDtypeStruct((late, units), jnp.float32), grad_shape, partial_shape),
        (held, held, vmem),
        [
            space(total, blocks * width), space(units, blocks * width),
            space(rows, blocks * width), space(units, blocks * width),
            space(total, units, dtype=jnp.float32), space(rows, units), space(rows, units),
        ],
        blocks * (QUADS + 3) + 1 + QUADS, WEIGH[1], [smem] + [held] * 7,
        (after(place, product), *firsts, gathered[1], weight, hidden),
    )
    lasts = (core[1], others[1], swap(after(others[1], before), 1))
    product = product_of((gathered[1], *lasts), WEIGH[2])
    grads.append(settle(product))
    hidden_grad, partial = call(
        late_kernel, (grad_shape, partial_shape), (held, vmem),
        [
            space(late, blocks * width), space(units, blocks * width),
            space(late, units, dtype=jnp.float32),
            space(QUADS - 1, rows, units), space(QUADS - 1, rows, units),
        ],
        blocks * QUADS + 3 * (QUADS - 1), 1 << 20, [smem] + [held] * 6 + [vmem, held],
        (after(place, product), *lasts, weight, before, hidden, early_partial, early_grad),
        {8: 0},
    )
    down_grad = call(
        join_kernel, jax.ShapeDtypeStruct((units, cols), jnp.bfloat16), held, [space(units, cols)],
        6, 1 << 20, [held] * CHUNKS, grads,
    )

    def canonical(x):
        x = x.reshape(QUADS, EXPERTS, capacity, -1).transpose(1, 0, 2, 3)
        return x.reshape(context_count * capacity, -1)

    hidden_grad = canonical(hidden_grad)
    sums = partial[:, 0].reshape(QUADS, EXPERTS, capacity).transpose(1, 0, 2)
    sums = sums.reshape(context_count, 1, capacity)
    outgoing_sums = jnp.broadcast_to(sums, (context_count, tensor_count, capacity))
    returned = lax.all_to_all(
        outgoing_sums.reshape(context_count * tensor_count, capacity),
        ("ctx", "tp"), split_axis=0, concat_axis=0, tiled=True,
    )
    expert_sums = returned.reshape(EXPERTS, -1, capacity).sum(axis=1)
    gates_sent = gates.astype(jnp.bfloat16).astype(jnp.float32)
    route_grad = jnp.take(expert_sums.reshape(-1), position) / gates_sent
    logit_grad = gates * (route_grad - jnp.sum(gates * route_grad, axis=0, keepdims=True))
    return (hidden_grad, down_grad, logit_grad.T)


def solution(mesh):
    in_specs = (
        P(("dp", "ctx"), "tp"),
        P(("dp", "ctx"), None),
        P(("dp", "ctx"), None),
        P("dp", ("ctx", "tp")),
        P(("ctx", "tp"), "dp"),
    )
    out_specs = (P("dp", ("ctx", "tp")), P(("ctx", "tp"), "dp"), P(("dp", "ctx"), None))
    return jax.shard_map(local, mesh=mesh, in_specs=in_specs, out_specs=out_specs, check_vma=False)
```

```python
import functools

import jax
import jax.numpy as jnp
from jax import lax
from jax.experimental import pallas as pl
from jax.experimental.pallas import tpu as pltpu
from jax.sharding import PartitionSpec as P

EXPERTS = 8
TOP = 2
QUADS = 4
VMEM_LIMIT = 56 * 1024 * 1024
PRODUCT_LIMIT = 48 * 1024 * 1024
CHUNKS = 2
WEIGH = (1 << 20, 1 << 20, 18 * 10**9)


def compare_dot(a, b):
    return lax.dot_general(a, b, (((1,), (1,)), ((), ())), preferred_element_type=jnp.float32)


def slab_rows(capacity):
    return (capacity // 8 + 1) * 8


def pack_kernel(capacity, ids_ref, logits_ref, upstream_ref, packed_ref, position_ref, gates_ref):
    tokens = upstream_ref.shape[0]
    rows = packed_ref.shape[0]
    per_expert = rows // EXPERTS
    ids = [ids_ref[k : k + 1, :] for k in range(TOP)]
    expert = lax.broadcasted_iota(jnp.int32, (EXPERTS, tokens), 0)
    chosen = [(expert == ids[k]).astype(jnp.float32) for k in range(TOP)]
    before = (
        lax.broadcasted_iota(jnp.int32, (tokens, tokens), 0)
        < lax.broadcasted_iota(jnp.int32, (tokens, tokens), 1)
    ).astype(jnp.bfloat16)
    earlier = jnp.dot(
        (chosen[0] + chosen[1]).astype(jnp.bfloat16), before, preferred_element_type=jnp.float32
    )
    row = lax.broadcasted_iota(jnp.int32, (rows, tokens), 0)
    place = jnp.zeros((rows, tokens), jnp.float32)
    for k in range(TOP):
        slot = jnp.sum(earlier * chosen[k], axis=0, keepdims=True).astype(jnp.int32)
        gate = 1.0 / (1.0 + jnp.exp(logits_ref[1 - k : 2 - k, :] - logits_ref[k : k + 1, :]))
        place = place + jnp.where(row == ids[k] * per_expert + slot, gate, 0.0)
        position_ref[k : k + 1, :] = ids[k] * capacity + slot
        gates_ref[k : k + 1, :] = gate
    packed = jnp.dot(
        place.astype(jnp.bfloat16), upstream_ref[...], preferred_element_type=jnp.float32
    )
    packed_ref[...] = packed.astype(jnp.bfloat16)


def pack(ids, logits, upstream, capacity):
    tokens, cols = upstream.shape
    rows = EXPERTS * slab_rows(capacity)
    return pl.pallas_call(
        functools.partial(pack_kernel, capacity),
        out_shape=(
            jax.ShapeDtypeStruct((rows, cols), jnp.bfloat16),
            jax.ShapeDtypeStruct((TOP, tokens), jnp.int32),
            jax.ShapeDtypeStruct((TOP, tokens), jnp.float32),
        ),
        compiler_params=pltpu.CompilerParams(vmem_limit_bytes=VMEM_LIMIT),
        cost_estimate=pl.CostEstimate(
            flops=2 * rows * tokens * cols, bytes_accessed=2 * (rows + tokens) * cols, transcendentals=0
        ),
    )(ids, logits, upstream)


class Copies:
    def __init__(self, sems):
        self.sems, self.count = sems, 0

    def __call__(self, source, target):
        made = pltpu.make_async_copy(source, target, self.sems.at[self.count])
        self.count += 1
        made.start()
        return made


def spans(size, count):
    return [slice(i * size, (i + 1) * size) for i in range(count)]


def wait(copies):
    for made in copies:
        made.wait()


def load_rows(copy, pieces, full):
    rows, blocks = full.shape[0] // len(pieces), pieces[0].shape[0]
    columns = spans(full.shape[1] // blocks, blocks)
    return [
        [copy(piece.at[j, 0:rows, :], full.at[at, column]) for j, column in enumerate(columns)]
        for piece, at in zip(pieces, spans(rows, len(pieces)))
    ]


def load_weight(copy, weight_ref, start, side):
    blocks = weight_ref.shape[0]
    width = side.shape[1] // blocks
    return [
        copy(weight_ref.at[j, :, start : start + width], side.at[:, column])
        for j, column in enumerate(spans(width, blocks))
    ]


def product_kernel(p0, p1, p2, p3, hidden_t_ref, product_ref, full, hidden_t, product, sems):
    copy = Copies(sems)
    blocks, _, width = product.shape
    rows = full.shape[0] // QUADS
    columns = spans(width, blocks)
    first = [copy(hidden_t_ref, hidden_t)]
    loads = [
        [
            copy(piece.at[j, 0:rows, :], full.at[at, column])
            for piece, at in zip((p0, p1, p2, p3), spans(rows, QUADS))
        ]
        for j, column in enumerate(columns)
    ]
    wait(first)
    stores = []
    for j, column in enumerate(columns):
        wait(loads[j])
        result = jnp.dot(hidden_t[...], full[:, column], preferred_element_type=jnp.float32)
        product[j] = result.astype(jnp.bfloat16)
        stores.append(copy(product.at[j], product_ref.at[j]))
    wait(stores)


def row_sums(x):
    lanes = 128
    folded = sum(x[:, at] for at in spans(lanes, x.shape[1] // lanes))
    return lax.dot_general(
        jnp.ones((8, lanes), jnp.float32), folded, (((1,), (1,)), ((), ())),
        precision=lax.Precision.HIGHEST, preferred_element_type=jnp.float32,
    )


def early_kernel(
    place_ref, p0, p1, p2, p3, n0, weight_ref, hidden_ref,
    before_ref, grad_ref, partial_ref,
    full, side, next_full, next_side, total, hidden, grad, sems,
):
    copy = Copies(sems)
    rows = next_full.shape[0]
    width = full.shape[1] // weight_ref.shape[0]
    sides = load_weight(copy, weight_ref, 0, side)
    loads = load_rows(copy, (p0, p1, p2, p3), full)
    sides_next = load_weight(copy, weight_ref, width, next_side)
    loads_next = load_rows(copy, (n0,), next_full)[0] + [copy(hidden_ref.at[0], hidden)]
    stores = []
    wait(sides)
    for i, at in enumerate(spans(rows, QUADS)):
        wait(loads[i])
        total[at, :] = compare_dot(full[at, :], side[...])
        if i:
            to = slice((i - 1) * rows, i * rows)
            stores.append(copy(total.at[at, :], before_ref.at[to, :]))
    wait(sides_next + loads_next)
    proj = total[:rows, :] + compare_dot(next_full[...], next_side[...])
    owner = place_ref[0]
    partial_ref[...] = jnp.zeros(partial_ref.shape, jnp.float32)
    partial_ref[owner] = row_sums(hidden[...].astype(jnp.float32) * proj)
    grad[...] = proj.astype(jnp.bfloat16)
    stores.append(copy(grad, grad_ref.at[owner]))
    wait(stores)


def late_kernel(
    place_ref, p1, p2, p3, weight_ref, before_ref, hidden_ref, early_partial_ref, early_grad,
    grad_ref, partial_ref, full, side, total, hidden, grad, sems,
):
    copy = Copies(sems)
    late = QUADS - 1
    rows = full.shape[0] // late
    width = full.shape[1] // weight_ref.shape[0]
    sides = load_weight(copy, weight_ref, width, side)
    loads = load_rows(copy, (p1, p2, p3), full)
    for i, at in enumerate(spans(rows, late)):
        loads[i].append(copy(before_ref.at[at, :], total.at[at, :]))
        loads[i].append(copy(hidden_ref.at[i + 1], hidden.at[i]))
    partial_ref[...] = early_partial_ref[...]
    wait(sides)
    stores = []
    for i, at in enumerate(spans(rows, late)):
        wait(loads[i])
        proj = total[at, :] + compare_dot(full[at, :], side[...])
        owner = jnp.bitwise_xor(place_ref[0], i + 1)
        partial_ref[owner] = row_sums(hidden[i].astype(jnp.float32) * proj)
        grad[i] = proj.astype(jnp.bfloat16)
        stores.append(copy(grad.at[i], grad_ref.at[owner]))
    wait(stores)


def join_kernel(a_ref, b_ref, out_ref, whole, sems):
    copy = Copies(sems)
    columns, parts = spans(a_ref.shape[1], CHUNKS), spans(a_ref.shape[0] // 2, 2)
    loads = [
        [copy(ref.at[at, :], whole.at[at, c]) for ref, c in zip((a_ref, b_ref), columns)]
        for at in parts
    ]
    stores = []
    for made, at in zip(loads, parts):
        wait(made)
        stores.append(copy(whole.at[at, :], out_ref.at[at, :]))
    wait(stores)


def after(x, *others):
    return lax.optimization_barrier((x,) + others)[0]


def local(upstream, router_logits, expert_ids, hidden_saved, down_weight):
    tokens, cols = upstream.shape
    tensor_count = lax.axis_size("tp")
    context_count = lax.axis_size("ctx")
    data_count = lax.axis_size("dp")
    capacity = hidden_saved.shape[0] // context_count
    units = hidden_saved.shape[1]
    rows = EXPERTS * capacity
    total = QUADS * rows
    quad = lax.rem(lax.axis_index("ctx"), QUADS)

    packed, position, gates = pack(expert_ids.T, router_logits.T, upstream, capacity)
    outgoing = packed.reshape(EXPERTS, slab_rows(capacity), cols)
    groups = [[q + QUADS * e for e in range(EXPERTS)] for q in range(QUADS)]
    received = lax.all_to_all(
        outgoing, "ctx", split_axis=0, concat_axis=0, tiled=True, axis_index_groups=groups
    )
    own_rows = received[:, :capacity].reshape(rows, cols)

    def swap(x, bit):
        return lax.ppermute(x, "ctx", [(c, c ^ bit) for c in range(context_count)])

    quads = hidden_saved.reshape(EXPERTS, QUADS, capacity, units).transpose(1, 0, 2, 3)
    quads = quads.reshape(QUADS, rows, units)
    hidden = jnp.stack(
        [
            lax.dynamic_index_in_dim(quads, jnp.bitwise_xor(quad, i), 0, keepdims=False)
            for i in range(QUADS)
        ]
    )

    hidden_t = hidden.reshape(total, units).T
    weight = lax.all_gather(down_weight, "dp", axis=0, tiled=False)
    width = cols // CHUNKS
    sent = [own_rows[:, column] for column in spans(width, CHUNKS)]
    sent[0] = after(sent[0], hidden, hidden_t)
    gathered = [lax.all_gather(x, "tp", axis=0, tiled=False) for x in sent]
    others = [swap(x, 2) for x in gathered]
    core = [swap(after(x, others[0], *gathered), 1) for x in gathered]
    last_others = swap(after(others[0], *gathered), 1)
    firsts = (gathered[0], core[0], others[0], last_others)

    place = quad.astype(jnp.int32).reshape(1)
    blocks = data_count
    held = pl.BlockSpec(memory_space=pltpu.HBM)
    vmem = pl.BlockSpec(memory_space=pltpu.VMEM)
    smem = pl.BlockSpec(memory_space=pltpu.SMEM)

    def space(*shape, dtype=jnp.bfloat16):
        return pltpu.VMEM(shape, dtype)

    def call(
        kernel, outputs, out_specs, scratch, copies, weigh, specs, inputs, aliases={}, limit=VMEM_LIMIT
    ):
        return pl.pallas_call(
            kernel,
            out_shape=outputs,
            in_specs=specs,
            out_specs=out_specs,
            scratch_shapes=scratch + [pltpu.SemaphoreType.DMA((copies,))],
            input_output_aliases=aliases,
            compiler_params=pltpu.CompilerParams(vmem_limit_bytes=limit),
            cost_estimate=pl.CostEstimate(
                flops=weigh, bytes_accessed=1 << 20, transcendentals=0
            ),
        )(*inputs)

    def product_of(pieces, weigh):
        return call(
            product_kernel, jax.ShapeDtypeStruct((blocks, units, width), jnp.bfloat16), held,
            [space(total, blocks * width), space(units, total), space(blocks, units, width)],
            1 + blocks * (QUADS + 1), weigh, [held] * 5, (*pieces, hidden_t),
            limit=PRODUCT_LIMIT,
        )

    def settle(product):
        return lax.psum_scatter(product, "dp", scatter_dimension=0, tiled=False)

    grad_shape = jax.ShapeDtypeStruct((QUADS, rows, units), jnp.bfloat16)
    partial_shape = jax.ShapeDtypeStruct((QUADS, 8, rows), jnp.float32)
    late = total - rows
    product = product_of(firsts, WEIGH[0])
    grads = [settle(product)]
    before, early_grad, early_partial = call(
        early_kernel, (jax.ShapeDtypeStruct((late, units), jnp.float32), grad_shape, partial_shape),
        (held, held, vmem),
        [
            space(total, blocks * width), space(units, blocks * width),
            space(rows, blocks * width), space(units, blocks * width),
            space(total, units, dtype=jnp.float32), space(rows, units), space(rows, units),
        ],
        blocks * (QUADS + 3) + 1 + QUADS, WEIGH[1], [smem] + [held] * 7,
        (after(place, product), *firsts, gathered[1], weight, hidden),
    )
    lasts = (core[1], others[1], swap(after(others[1], before), 1))
    product = product_of((gathered[1], *lasts), WEIGH[2])
    grads.append(settle(product))
    hidden_grad, partial = call(
        late_kernel, (grad_shape, partial_shape), (held, vmem),
        [
            space(late, blocks * width), space(units, blocks * width),
            space(late, units, dtype=jnp.float32),
            space(QUADS - 1, rows, units), space(QUADS - 1, rows, units),
        ],
        blocks * QUADS + 3 * (QUADS - 1), 1 << 20, [smem] + [held] * 6 + [vmem, held],
        (after(place, product), *lasts, weight, before, hidden, early_partial, early_grad),
        {8: 0},
    )
    down_grad = call(
        join_kernel, jax.ShapeDtypeStruct((units, cols), jnp.bfloat16), held, [space(units, cols)],
        6, 1 << 20, [held] * CHUNKS, grads,
    )

    def canonical(x):
        x = x.reshape(QUADS, EXPERTS, capacity, -1).transpose(1, 0, 2, 3)
        return x.reshape(context_count * capacity, -1)

    hidden_grad = canonical(hidden_grad)
    sums = partial[:, 0].reshape(QUADS, EXPERTS, capacity).transpose(1, 0, 2)
    sums = sums.reshape(context_count, 1, capacity)
    outgoing_sums = jnp.broadcast_to(sums, (context_count, tensor_count, capacity))
    returned = lax.all_to_all(
        outgoing_sums.reshape(context_count * tensor_count, capacity),
        ("ctx", "tp"), split_axis=0, concat_axis=0, tiled=True,
    )
    expert_sums = returned.reshape(EXPERTS, -1, capacity).sum(axis=1)
    gates_sent = gates.astype(jnp.bfloat16).astype(jnp.float32)
    route_grad = jnp.take(expert_sums.reshape(-1), position) / gates_sent
    logit_grad = gates * (route_grad - jnp.sum(gates * route_grad, axis=0, keepdims=True))
    return (hidden_grad, down_grad, logit_grad.T)


def solution(mesh):
    in_specs = (
        P(("dp", "ctx"), "tp"),
        P(("dp", "ctx"), None),
        P(("dp", "ctx"), None),
        P("dp", ("ctx", "tp")),
        P(("ctx", "tp"), "dp"),
    )
    out_specs = (P("dp", ("ctx", "tp")), P(("ctx", "tp"), "dp"), P(("dp", "ctx"), None))
    return jax.shard_map(local, mesh=mesh, in_specs=in_specs, out_specs=out_specs, check_vma=False)
```
